32 devices in a mesh: mesh: 8 (over z, x), bg: 4 (over y, core).
Axes of the slice: x: 2, y: 2, z: 4, core: 2. Of those that a mesh axis runs over, the one named last changes fastest.
Arguments:
- displacement: float32 [3, 32, 16, 128], P(None, 'mesh', 'bg'), may hold values from -0.4 to 0.4
- bg_coef: float32 [8, 524288], P(None, ('mesh', 'bg')), may hold values from -0.3 to 0.3
- query_elem: int32 [32, 32, 544], P(('mesh', 'bg')), may hold values from 0 to 16383
- query_point: int32 [32, 32, 544], P(('mesh', 'bg')), may hold values from 0 to 6912, as said below
- query_coord: float32 [32, 32, 3, 544], P(('mesh', 'bg')), may hold values from 0 to 1
Outputs:
- new_displacement: float32 [3, 32, 16, 128], P(None, 'mesh', 'bg')
- line_coeffs: float32 [2, 5], replicated
The draws below stay inside these ranges and needn't reach their ends.
Inputs may be any that keep to these rules, and one draw needn't show every extreme that they name: `query_point`: in each row every quadrature point 0 to 6911 of the row's device fills exactly one slot; all other slots hold 6912 and are empty. In every draw some owner's bucket is full in every row.
All inputs are finite; a program needn't handle non-finite values.
Results may differ from the reference program's by a relative error of at most 0.0003.
Values sent between devices are 32-bit elements; how exact they have to be, the bound alone decides.
A program may use at most 64 MiB of HBM per device.

```python
import jax
import jax.numpy as jnp
import numpy as np
from jax import lax

EX = 64
EY = 2
EZ = 2
BGE_DEV = 16384
PASSES = 2
LS_STEPS = 4
QPTS_DEV = 6912
CAP = 544
NXN = 128
NYN = 16
NZN = 32
BGE = 524288
NELEM = 8192
N_MESH = 8
N_BG = 4
DEVICES = 32


def draw_displacement(key, part):
    shape_full = (3, NZN, NYN, NXN)
    depth = jnp.arange(NZN, dtype=jnp.float32)[None, :, None, None] / NZN
    amplitude = 0.03 * (1.0 + 2.0 * depth)
    noise = jax.random.truncated_normal(key, -4.0, 4.0, shape_full, jnp.float32)
    return noise * amplitude


def draw_query_point(key, part):
    slot_positions = DEVICES * CAP
    heavy = jax.random.randint(jax.random.fold_in(key, 1), (), 0, DEVICES)
    extra_credit = jax.random.randint(jax.random.fold_in(key, 2), (DEVICES,), 0, 4) * 32
    owning_device = jnp.arange(slot_positions, dtype=jnp.int32) // CAP

    def one_row(row_lookup_key):
        quality_level = jax.random.randint(jax.random.fold_in(row_lookup_key, 3), (slot_positions,), 0, 64) + extra_credit[owning_device]
        quality_level = jnp.where(owning_device == heavy, 200, quality_level)
        score = quality_level * slot_positions + jnp.arange(slot_positions, dtype=jnp.int32)
        order = jnp.argsort(-score)
        chosen = order[:QPTS_DEV]
        labels = jax.random.permutation(jax.random.fold_in(row_lookup_key, 4), QPTS_DEV).astype(jnp.int32)
        return jnp.full((slot_positions,), QPTS_DEV, jnp.int32).at[chosen].set(labels)
    rows = jax.vmap(one_row)(jax.random.split(jax.random.fold_in(key, 5), DEVICES))
    return rows.reshape(DEVICES, DEVICES, CAP)


def with_ends(entries, stream_key, least, top_value):
    shape = entries.shape
    index_at = [jax.random.randint(jax.random.fold_in(stream_key, axis), (), 0, shape[axis]) for axis in range(len(shape))]
    entries = entries.at[tuple(index_at)].set(least)
    longest = shape.index(max(shape))
    index_at[longest] = (index_at[longest] + 1) % shape[longest]
    return entries.at[tuple(index_at)].set(top_value)


def block_levels(key, extent, cuts, smallest, high):
    level, own = 1.0, jax.random.fold_in(key, 6)
    for axis_at, blocks in cuts:
        steps = jnp.exp(jax.random.uniform(jax.random.fold_in(own, axis_at), (blocks,), jnp.float32, smallest / len(cuts), high / len(cuts)))
        level = level * jnp.repeat(steps, extent[axis_at] // blocks).reshape([-1 if axis == axis_at else 1 for axis in range(len(extent))])
    return level


def setup_inputs(seed: int = 0) -> dict:
    arg_keys = jax.random.split(jax.random.key(seed), 6)
    return {
        "displacement": draw_displacement(jax.random.fold_in(arg_keys[5], 71), 0),
        "bg_coef": jnp.clip(jax.random.uniform(arg_keys[1], (8, BGE), jnp.float32, -0.3, 0.3) * block_levels(arg_keys[1], (8, BGE), ((1, 32),), -0.4, 0.0), -0.3, 0.3),
        "query_elem": with_ends(jax.random.randint(arg_keys[2], (DEVICES, DEVICES, CAP), 0, BGE_DEV), jax.random.fold_in(arg_keys[2], 1), 0, BGE_DEV - 1).astype(jnp.int32),
        "query_point": draw_query_point(jax.random.fold_in(arg_keys[5], 71), 0),
        "query_coord": jnp.clip(1.0 * jax.random.uniform(arg_keys[4], (DEVICES, DEVICES, 3, CAP), jnp.float32) ** block_levels(arg_keys[4], (DEVICES, DEVICES, 3, CAP), ((0, 32),), -0.2, 0.2), 0.0, 1.0),
    }


GAUSS_POINTS = np.array([0.5 - 0.5 * np.sqrt(0.6), 0.5, 0.5 + 0.5 * np.sqrt(0.6)])
GAUSS_WEIGHTS = np.array([5.0 / 18.0, 8.0 / 18.0, 5.0 / 18.0])

def basis_tables(elements, periodic):
    node_count = 2 * elements if periodic else 2 * elements + 1
    values = np.zeros((node_count, 3 * elements))
    slopes = np.zeros((node_count, 3 * elements))
    points = GAUSS_POINTS
    shape_values = [2.0 * (points - 0.5) * (points - 1.0), -4.0 * points * (points - 1.0), 2.0 * points * (points - 0.5)]
    shape_slopes = [4.0 * points - 3.0, 4.0 - 8.0 * points, 4.0 * points - 1.0]
    for offset in range(3):
        node_rows = (2 * np.arange(elements) + offset) % node_count
        for gauss_index in range(3):
            columns = 3 * np.arange(elements) + gauss_index
            values[node_rows, columns] += shape_values[offset][gauss_index]
            slopes[node_rows, columns] += shape_slopes[offset][gauss_index]
    return (jnp.asarray(values, dtype=jnp.float32), jnp.asarray(slopes, dtype=jnp.float32))

def quad_weights(z_elems, y_elems, x_elems):
    along_z = jnp.asarray(np.tile(GAUSS_WEIGHTS, z_elems), dtype=jnp.float32)
    along_y = jnp.asarray(np.tile(GAUSS_WEIGHTS, y_elems), dtype=jnp.float32)
    along_x = jnp.asarray(np.tile(GAUSS_WEIGHTS, x_elems), dtype=jnp.float32)
    return along_z[:, None, None] * along_y[None, :, None] * along_x[None, None, :]

def gradients(node_field, tables):
    z_value, z_slope, y_value, y_slope, value_along_x, x_slope = tables
    highest = lax.Precision.HIGHEST
    value_z = jnp.einsum('czyx,zk->ckyx', node_field, z_value, precision=highest)
    slope_z = jnp.einsum('czyx,zk->ckyx', node_field, z_slope, precision=highest)
    value_zy = jnp.einsum('ckyx,yl->cklx', value_z, y_value, precision=highest)
    slope_y = jnp.einsum('ckyx,yl->cklx', value_z, y_slope, precision=highest)
    slope_zy = jnp.einsum('ckyx,yl->cklx', slope_z, y_value, precision=highest)
    deriv_x = jnp.einsum('cklx,xm->cklm', value_zy, x_slope, precision=highest)
    deriv_y = jnp.einsum('cklx,xm->cklm', slope_y, value_along_x, precision=highest)
    deriv_z = jnp.einsum('cklx,xm->cklm', slope_zy, value_along_x, precision=highest)
    return jnp.stack([deriv_x, deriv_y, deriv_z], axis=1)

def identity_block():
    return jnp.eye(3, dtype=jnp.float32)[:, :, None, None, None]

def gram(left_part, right_part):
    return lax.optimization_barrier(jnp.sum(left_part[:, :, None] * right_part[:, None, :], axis=0))

def energy(node_field, tables, target_size_scale, weights):
    jacobian = gradients(node_field, tables) + identity_block()
    strain = gram(jacobian, jacobian) * target_size_scale - identity_block()
    return jnp.sum(weights * lax.optimization_barrier(jnp.sum(strain * strain, axis=(0, 1))))

def line_terms(node_field, direction, tables, target_size_scale, weights):
    jacobian = gradients(node_field, tables) + identity_block()
    motion = gradients(direction, tables)
    strain_zero = gram(jacobian, jacobian) * target_size_scale - identity_block()
    mixed = gram(jacobian, motion)
    strain_one = (mixed + jnp.swapaxes(mixed, 0, 1)) * target_size_scale
    strain_two = gram(motion, motion) * target_size_scale

    def weighted(first_part, latter_portion):
        return jnp.sum(weights * lax.optimization_barrier(jnp.sum(first_part * latter_portion, axis=(0, 1))))
    zero_zero = weighted(strain_zero, strain_zero)
    zero_one = weighted(strain_zero, strain_one)
    zero_two = weighted(strain_zero, strain_two)
    one_two = weighted(strain_one, strain_two)
    two_two = weighted(strain_two, strain_two)
    gauss_newton = weighted(strain_one, strain_one)
    return (zero_zero, 2.0 * zero_one, gauss_newton + 2.0 * zero_two, 2.0 * one_two, two_two, gauss_newton)

def line_search(terms):
    const_term, linear, quadratic, cubic_term, quartic, gauss_newton = terms
    step_len = jnp.zeros((), jnp.float32)
    for search_turn in range(LS_STEPS):
        slope = linear + step_len * (2.0 * quadratic + step_len * (3.0 * cubic_term + step_len * 4.0 * quartic))
        curvature = 2.0 * quadratic + step_len * (6.0 * cubic_term + step_len * 12.0 * quartic)
        step_len = step_len - slope / jnp.maximum(curvature, gauss_newton + 1e-06)
    return step_len

def inverse_square(coefs, coords):
    along_x = coords[:, 0]
    along_y = coords[:, 1]
    along_z = coords[:, 2]
    summed = jnp.zeros_like(along_x)
    for corner in range(8):
        weight_x = along_x if corner & 1 else 1.0 - along_x
        weight_y = along_y if corner & 2 else 1.0 - along_y
        weight_z = along_z if corner & 4 else 1.0 - along_z
        summed = summed + weight_x * weight_y * weight_z * coefs[:, corner]
    return jnp.exp(-2.0 * summed)

def reference(displacement, bg_coef, query_elem, query_point, query_coord):
    devices = N_MESH * N_BG
    offsets = (jnp.arange(devices, dtype=jnp.int32) * BGE_DEV)[:, None]

    def per_source(items):
        elem_ids, point_ids, coords = items
        coefs = jnp.stack([jnp.take(bg_coef[corner], elem_ids + offsets) for corner in range(8)], axis=1)
        found_vals = inverse_square(coefs, coords)
        return jnp.zeros((QPTS_DEV,), jnp.float32).at[point_ids.reshape(-1)].set(found_vals.reshape(-1), mode='drop')
    spread = lax.map(per_source, (query_elem, query_point, query_coord))
    spread = spread.reshape(N_MESH, N_BG, 3 * EZ, 3 * EY, 3 * EX).transpose(0, 2, 1, 3, 4)
    target_size_scale = spread.reshape(N_MESH * 3 * EZ, N_BG * 3 * EY, 3 * EX)
    weights = quad_weights(EZ * N_MESH, EY * N_BG, EX)
    tables = basis_tables(EZ * N_MESH, True) + basis_tables(EY * N_BG, True) + basis_tables(EX, True)

    def total_energy(values):
        return energy(values, tables, target_size_scale, weights)
    node_field = displacement
    history = []
    for newton_pass in range(PASSES):
        direction = -jax.grad(total_energy)(node_field)
        line_poly = line_terms(node_field, direction, tables, target_size_scale, weights)
        step_len = line_search(line_poly)
        node_field = node_field + step_len * direction
        history.append(jnp.stack(line_poly[:5]) / NELEM)
    return (node_field, jnp.stack(history))
```

```python
import functools

import jax
import jax.numpy as jnp
import numpy as np
from jax import lax
from jax.experimental import pallas as pl
from jax.experimental.pallas import tpu as pltpu
from jax.sharding import PartitionSpec as P

PASSES = 2
LS_STEPS = 4
ROW = 8
LO = 256

GAUSS_POINTS = np.array([0.5 - 0.5 * np.sqrt(0.6), 0.5, 0.5 + 0.5 * np.sqrt(0.6)])
GAUSS_WEIGHTS = np.array([5.0 / 18.0, 8.0 / 18.0, 5.0 / 18.0])
MESH = pl.DeviceIdType.MESH
HIGHEST = lax.Precision.HIGHEST


def basis_tables(elements, periodic):
    node_count = 2 * elements if periodic else 2 * elements + 1
    values = np.zeros((node_count, 3 * elements))
    slopes = np.zeros((node_count, 3 * elements))
    points = GAUSS_POINTS
    shape_values = [
        2.0 * (points - 0.5) * (points - 1.0),
        -4.0 * points * (points - 1.0),
        2.0 * points * (points - 0.5),
    ]
    shape_slopes = [4.0 * points - 3.0, 4.0 - 8.0 * points, 4.0 * points - 1.0]
    for offset in range(3):
        node_rows = (2 * np.arange(elements) + offset) % node_count
        for gauss_index in range(3):
            columns = 3 * np.arange(elements) + gauss_index
            values[node_rows, columns] += shape_values[offset][gauss_index]
            slopes[node_rows, columns] += shape_slopes[offset][gauss_index]
    return values, slopes


def round_up(value, unit):
    return -(-value // unit) * unit


def make_tables(ze, ye, xe):
    zv, zs = basis_tables(ze, False)
    yv, ys = basis_tables(ye, False)
    xv, xs = basis_tables(xe, True)
    nz, ny = zv.shape[0], yv.shape[0]
    qr, qx = 9 * ze * ye, 3 * xe
    qrp, qxp = round_up(qr, 8), round_up(qx, 128)

    def rows(tz, ty):
        out = np.zeros((qrp, nz, ROW))
        out[:qr, :, :ny] = np.einsum("zk,yl->klzy", tz, ty).reshape(qr, nz, ny)
        return out.reshape(qrp, nz * ROW)

    vv, vd, dv = rows(zv, yv), rows(zv, ys), rows(zs, yv)
    along_x = np.zeros((2 * xe, 2 * qxp))
    along_x[:, :qx] = xv
    along_x[:, qxp : qxp + qx] = xs
    weights = np.zeros((qrp, qxp))
    weights[:qr, :qx] = np.einsum(
        "z,y,x->zyx",
        np.tile(GAUSS_WEIGHTS, ze),
        np.tile(GAUSS_WEIGHTS, ye),
        np.tile(GAUSS_WEIGHTS, xe),
    ).reshape(qr, qx)
    tables = (
        along_x,
        along_x.T,
        vv,
        np.concatenate([vd, dv], axis=0),
        vv.T,
        np.concatenate([vd.T, dv.T], axis=1),
        weights,
    )
    return tuple(np.ascontiguousarray(t).astype(np.float32) for t in tables)


def dot(a, b):
    return lax.dot_general(
        a, b, (((1,), (0,)), ((), ())), precision=HIGHEST, preferred_element_type=jnp.float32
    )


def kernel(
    dims,
    disp, coef, elem, point, coord, xt, xtt, vv, vdv, vvt, vdvt, wts,
    out, lc,
    query, arrived, answer, found, tab32, tab, scat, fld, grad,
    hy_send, hc_send, hz, hy, hc,
    ysend, csend, zrecv, yrecv, crecv, part, sums,
    q_send, q_recv, f_send, f_recv, h_send, h_recv, x_send, x_recv, a_send, a_recv,
):
    n_mesh, n_bg, nz, ny, qx = dims
    n = n_mesh * n_bg
    cap = elem.shape[1]
    his = coef.shape[1] // LO
    qrp, qxp = wts.shape
    zi, yi = lax.axis_index("mesh"), lax.axis_index("bg")
    me = zi * n_bg + yi

    def device(index):
        return (lax.div(index, n_bg), lax.rem(index, n_bg))

    def near(dz, dy):
        return (lax.rem(zi + n_mesh + dz, n_mesh), lax.rem(yi + n_bg + dy, n_bg))

    def remote(src, dst, ssem, rsem, target):
        return pltpu.make_async_remote_copy(
            src_ref=src, dst_ref=dst, send_sem=ssem, recv_sem=rsem,
            device_id=target, device_id_type=MESH,
        )

    def wait_bytes(ref, sem):
        pltpu.make_async_copy(ref, ref, sem).wait()

    barrier = pltpu.get_barrier_semaphore()

    def greet(d, carry):
        pl.semaphore_signal(
            barrier, inc=1, device_id=device(lax.rem(me + d, n)), device_id_type=MESH
        )
        return carry

    lax.fori_loop(1, n, greet, 0)

    def pack(o, carry):
        query[o, 0:1, :] = elem[pl.ds(o, 1), :].astype(jnp.float32)
        query[o, 1:4, :] = coord[o]
        return carry

    lax.fori_loop(0, n, pack, 0)
    for c in range(3):
        for z in range(nz - 1):
            hy_send[c, z : z + 1, :] = disp[c, z, 0:1, :]
        hc_send[c : c + 1, :] = disp[c, 0, 0:1, :]
    pl.semaphore_wait(barrier, n - 1)

    def send_query(d, carry):
        target = lax.rem(me + d, n)
        remote(
            query.at[target], arrived.at[d], q_send, q_recv.at[d], device(target)
        ).start()
        return carry

    lax.fori_loop(1, n, send_query, 0)
    halo = [
        remote(disp.at[:, 0], hz, h_send.at[0], h_recv.at[0], near(-1, 0)),
        remote(hy_send, hy, h_send.at[1], h_recv.at[1], near(0, -1)),
        remote(hc_send, hc, h_send.at[2], h_recv.at[2], near(-1, -1)),
    ]
    for copy in halo:
        copy.start()

    for h in range(his):
        tab32[8 * h : 8 * h + 8, :] = coef[:, LO * h : LO * h + LO]
    whole = tab32[...]
    top = whole.astype(jnp.bfloat16)
    tab[:, :LO] = top
    tab[:, LO:] = (whole - top.astype(jnp.float32)).astype(jnp.bfloat16)
    arrived[0] = query[me]

    corner = lax.broadcasted_iota(jnp.int32, (8, cap), 0)
    lo_rows = lax.broadcasted_iota(jnp.int32, (LO, cap), 0)

    def serve(d):
        ids = arrived[d, 0:1, :].astype(jnp.int32)
        hi = lax.shift_right_logical(ids, LO.bit_length() - 1)
        lo = lax.bitwise_and(ids, LO - 1)
        one_hot = jnp.where(lo_rows == lo, 1.0, 0.0).astype(jnp.bfloat16)
        one_hot = jnp.concatenate([one_hot, one_hot], axis=0)
        rows = lax.dot_general(
            tab[...], one_hot, (((1,), (0,)), ((), ())), preferred_element_type=jnp.float32
        )
        hi8 = jnp.broadcast_to(hi, (8, cap))
        chosen = rows[0:8]
        for h in range(1, his):
            chosen = jnp.where(hi8 == h, rows[8 * h : 8 * h + 8], chosen)
        x, y, z = (arrived[d, j : j + 1, :] for j in (1, 2, 3))
        ax = jnp.where((corner & 1) != 0, x, 1.0 - x)
        ay = jnp.where((corner & 2) != 0, y, 1.0 - y)
        az = jnp.where((corner & 4) != 0, z, 1.0 - z)
        lsize = jnp.sum(ax * ay * az * chosen, axis=0, keepdims=True)
        return jnp.exp(-2.0 * lsize)

    found[me] = serve(0)

    def serve_remote(d, carry):
        source = lax.rem(me + n - d, n)
        remote(query.at[0], arrived.at[d], q_send, q_recv.at[d], device(source)).wait_recv()
        answer[d] = serve(d)
        remote(answer.at[d], found.at[me], f_send, f_recv, device(source)).start()
        return carry

    lax.fori_loop(1, n, serve_remote, 0)

    for copy in halo:
        copy.wait()
    fld[...] = jnp.zeros_like(fld)
    for c in range(3):
        for z in range(nz - 1):
            fld[c, z, 0 : ny - 1, :] = disp[c, z]
            fld[c, z, ny - 1 : ny, :] = hy[c, z : z + 1, :]
        fld[c, nz - 1, 0 : ny - 1, :] = hz[c]
        fld[c, nz - 1, ny - 1 : ny, :] = hc[c : c + 1, :]

    def derivatives(flat):
        along = dot(flat, xt[...])
        result = []
        for c in range(3):
            rows = along[c * nz * ROW : (c + 1) * nz * ROW]
            dx = dot(vv[...], rows[:, qxp:])
            dyz = dot(vdv[...], rows[:, :qxp])
            result.append([dx, dyz[:qrp], dyz[qrp:]])
        return result

    jac = derivatives(fld[...].reshape(3 * nz * ROW, -1))
    for c in range(3):
        jac[c][c] = jac[c][c] + 1.0

    wait_bytes(found.at[pl.ds(0, n - 1)], f_recv)
    scat[...] = jnp.zeros_like(scat)
    hi_rows = lax.broadcasted_iota(jnp.int32, (qrp, cap), 0)
    qx_rows = lax.broadcasted_iota(jnp.int32, (qxp, cap), 0)

    def place(o, carry):
        p = point[pl.ds(o, 1), :].astype(jnp.float32)
        hi = jnp.floor((p + 0.5) * (1.0 / qx))
        lo = (p - hi * qx).astype(jnp.int32)
        mine = hi_rows == hi.astype(jnp.int32)
        value = found[o]
        pieces = []
        for _ in range(3):
            piece = value.astype(jnp.bfloat16).astype(jnp.float32)
            value = value - piece
            pieces.append(jnp.where(mine, piece, 0.0).astype(jnp.bfloat16))
        left = jnp.concatenate(pieces, axis=0)
        right = jnp.where(qx_rows == lo, 1.0, 0.0).astype(jnp.bfloat16)
        scat[...] += lax.dot_general(
            left, right, (((1,), (1,)), ((), ())), preferred_element_type=jnp.float32
        )
        return carry

    lax.fori_loop(0, n, place, 0)
    scale = scat[:qrp] + scat[qrp : 2 * qrp] + scat[2 * qrp :]
    weights = wts[...]
    scale = jnp.where(weights > 0.0, scale, 0.0)

    pairs = [(k, l) for k in range(3) for l in range(k, 3)]

    def gram(a, b):
        return {
            (k, l): a[0][k] * b[0][l] + a[1][k] * b[1][l] + a[2][k] * b[2][l]
            for k, l in (pairs if a is b else [(k, l) for k in range(3) for l in range(3)])
        }

    def inner(a, b):
        diag = sum(a[k, k] * b[k, k] for k in range(3))
        off = a[0, 1] * b[0, 1] + a[0, 2] * b[0, 2] + a[1, 2] * b[1, 2]
        return jnp.sum(weights * (diag + 2.0 * off), axis=0, keepdims=True)

    for turn in range(PASSES):
        gr = gram(jac, jac)
        r0 = {kl: gr[kl] * scale - (1.0 if kl[0] == kl[1] else 0.0) for kl in pairs}
        factor = (4.0 * weights) * scale
        for c in range(3):
            pulled = []
            for k in range(3):
                total = sum(r0[min(k, l), max(k, l)] * jac[c][l] for l in range(3))
                pulled.append(total * factor)
            by_value = dot(vdvt[...], jnp.concatenate([pulled[1], pulled[2]], axis=0))
            by_slope = dot(vvt[...], pulled[0])
            node = dot(jnp.concatenate([by_value, by_slope], axis=1), xtt[...])
            grad[turn, c] = node.reshape(nz, ROW, -1)

        for c in range(3):
            for side, y in enumerate((0, ny - 1)):
                for z in range(nz):
                    ysend[turn, side, c, z : z + 1, :] = grad[turn, c, z, y : y + 1, :]
                for zside, z in enumerate((0, nz - 1)):
                    csend[turn, 2 * zside + side, c : c + 1, :] = grad[turn, c, z, y : y + 1, :]
        copies = []
        for side, step in enumerate((-1, 1)):
            plane = (0, nz - 1)[side]
            copies.append((grad.at[turn, :, plane], zrecv.at[turn, 1 - side], near(step, 0)))
            copies.append((ysend.at[turn, side], yrecv.at[turn, 1 - side], near(0, step)))
            for other, ystep in enumerate((-1, 1)):
                index = 2 * side + other
                copies.append((csend.at[turn, index], crecv.at[turn, 3 - index], near(step, ystep)))
        copies = [
            remote(src, dst, x_send.at[8 * turn + i], x_recv.at[8 * turn + i], target)
            for i, (src, dst, target) in enumerate(copies)
        ]
        for copy in copies:
            copy.start()
        for copy in copies:
            copy.wait()
        for c in range(3):
            for side, z in enumerate((0, nz - 1)):
                grad[turn, c, z] += zrecv[turn, side, c]
            for side, y in enumerate((0, ny - 1)):
                for z in range(nz):
                    grad[turn, c, z, y : y + 1, :] += yrecv[turn, side, c, z : z + 1, :]
                for zside, z in enumerate((0, nz - 1)):
                    grad[turn, c, z, y : y + 1, :] += crecv[turn, 2 * zside + side, c : c + 1, :]

        direction = -grad[turn]
        move = derivatives(direction.reshape(3 * nz * ROW, -1))
        mixed = gram(jac, move)
        r1 = {(k, l): (mixed[k, l] + mixed[l, k]) * scale for k, l in pairs}
        mm = gram(move, move)
        r2 = {kl: mm[kl] * scale for kl in pairs}
        terms = [
            inner(r0, r0), inner(r0, r1), inner(r0, r2),
            inner(r1, r2), inner(r2, r2), inner(r1, r1),
        ]
        terms = jnp.concatenate(terms + [jnp.zeros((2, qxp), jnp.float32)], axis=0)
        mine = terms[:, :128]
        for lane in range(128, qxp, 128):
            mine = mine + terms[:, lane : lane + 128]
        part[turn] = mine
        sums[turn, me] = mine

        def share(d, carry, turn=turn):
            remote(
                part.at[turn], sums.at[turn, me], a_send.at[turn], a_recv.at[turn],
                device(lax.rem(me + d, n)),
            ).start()
            return carry

        lax.fori_loop(1, n, share, 0)
        wait_bytes(sums.at[turn, pl.ds(0, n - 1)], a_recv.at[turn])
        totals = jnp.sum(jnp.sum(sums[turn], axis=0), axis=1, keepdims=True)
        d00, d01, d02, d12, d22, gn = (
            jnp.broadcast_to(totals[i : i + 1], (1, 128)) for i in range(6)
        )
        c0, c1, c2, c3, c4 = d00, 2.0 * d01, gn + 2.0 * d02, 2.0 * d12, d22
        t = jnp.zeros((1, 128), jnp.float32)
        for _ in range(LS_STEPS):
            slope = c1 + t * (2.0 * c2 + t * (3.0 * c3 + t * 4.0 * c4))
            curvature = 2.0 * c2 + t * (6.0 * c3 + t * 12.0 * c4)
            t = t - slope / jnp.maximum(curvature, gn + 1e-06)
        count = n * (qrp // 9) * (qx // 3)
        for i, value in enumerate((c0, c1, c2, c3, c4)):
            lc[turn : turn + 1, i : i + 1] = value[:, :1] / count
        fld[...] = fld[...] + t.reshape(1, 1, 1, 128) * direction
        if turn + 1 < PASSES:
            wide = t[:, :1]
            jac = [[jac[c][k] + wide * move[c][k] for k in range(3)] for c in range(3)]

    for c in range(3):
        for z in range(nz - 1):
            out[c, z] = fld[c, z, 0 : ny - 1, :]

    wait_bytes(query.at[pl.ds(0, n - 1)], q_send)
    wait_bytes(answer.at[pl.ds(0, n - 1)], f_send)
    for turn in range(PASSES):
        wait_bytes(sums.at[turn, pl.ds(0, n - 1)], a_send.at[turn])


def shards(mesh_shape, displacement, bg_coef, query_elem, query_point, query_coord):
    n_mesh, n_bg = mesh_shape
    n = n_mesh * n_bg
    _, nz0, ny0, nx = displacement.shape
    ze, ye, xe = nz0 // 2, ny0 // 2, nx // 2
    nz, ny = nz0 + 1, ny0 + 1
    assert ny <= ROW and nx == 128
    cap = query_elem.shape[2]
    tables = make_tables(ze, ye, xe)
    qrp, qxp = tables[-1].shape
    his = bg_coef.shape[1] // LO
    f32 = jnp.float32
    dims = (n_mesh, n_bg, nz, ny, 3 * xe)
    vmem = pl.BlockSpec(memory_space=pltpu.VMEM)
    dma = pltpu.SemaphoreType.DMA
    scratch = [
        pltpu.VMEM((n, 4, cap), f32),
        pltpu.VMEM((n, 4, cap), f32),
        pltpu.VMEM((n, 1, cap), f32),
        pltpu.VMEM((n, 1, cap), f32),
        pltpu.VMEM((8 * his, LO), f32),
        pltpu.VMEM((8 * his, 2 * LO), jnp.bfloat16),
        pltpu.VMEM((3 * qrp, qxp), f32),
        pltpu.VMEM((3, nz, ROW, nx), f32),
        pltpu.VMEM((PASSES, 3, nz, ROW, nx), f32),
        pltpu.VMEM((3, nz0, nx), f32),
        pltpu.VMEM((3, nx), f32),
        pltpu.VMEM((3, ny0, nx), f32),
        pltpu.VMEM((3, nz0, nx), f32),
        pltpu.VMEM((3, nx), f32),
        pltpu.VMEM((PASSES, 2, 3, nz, nx), f32),
        pltpu.VMEM((PASSES, 4, 3, nx), f32),
        pltpu.VMEM((PASSES, 2, 3, ROW, nx), f32),
        pltpu.VMEM((PASSES, 2, 3, nz, nx), f32),
        pltpu.VMEM((PASSES, 4, 3, nx), f32),
        pltpu.VMEM((PASSES, 8, 128), f32),
        pltpu.VMEM((PASSES, n, 8, 128), f32),
        dma, dma((n,)), dma, dma, dma((3,)), dma((3,)),
        dma((8 * PASSES,)), dma((8 * PASSES,)), dma((PASSES,)), dma((PASSES,)),
    ]
    out, lc = pl.pallas_call(
        functools.partial(kernel, dims),
        out_shape=(
            jax.ShapeDtypeStruct(displacement.shape, f32),
            jax.ShapeDtypeStruct((PASSES, 5), f32),
        ),
        in_specs=[vmem] * 12,
        out_specs=(vmem, vmem),
        scratch_shapes=scratch,
        compiler_params=pltpu.CompilerParams(
            collective_id=0, has_side_effects=True, vmem_limit_bytes=48 * 2**20
        ),
    )(
        displacement, bg_coef, query_elem[0], query_point[0], query_coord[0],
        *(jnp.asarray(t) for t in tables),
    )
    return out, lc


def solution(mesh):
    in_specs = (
        P(None, "mesh", "bg", None),
        P(None, ("mesh", "bg")),
        P(("mesh", "bg"), None, None),
        P(("mesh", "bg"), None, None),
        P(("mesh", "bg"), None, None, None),
    )
    out_specs = (P(None, "mesh", "bg", None), P())
    body = functools.partial(shards, (mesh.shape["mesh"], mesh.shape["bg"]))
    return jax.shard_map(body, mesh=mesh, in_specs=in_specs, out_specs=out_specs, check_vma=False)
```

```python
import functools

import jax
import jax.numpy as jnp
import ml_dtypes
import numpy as np
from jax import lax
from jax.experimental import pallas as pl
from jax.experimental.pallas import tpu as pltpu
from jax.sharding import PartitionSpec as P

PASSES = 2
LS_STEPS = 4
ROW = 8
LO = 256
GROUP = 4

GAUSS_POINTS = np.array([0.5 - 0.5 * np.sqrt(0.6), 0.5, 0.5 + 0.5 * np.sqrt(0.6)])
GAUSS_WEIGHTS = np.array([5.0 / 18.0, 8.0 / 18.0, 5.0 / 18.0])
MESH = pl.DeviceIdType.MESH


def basis_tables(elements, periodic):
    node_count = 2 * elements if periodic else 2 * elements + 1
    values = np.zeros((node_count, 3 * elements))
    slopes = np.zeros((node_count, 3 * elements))
    points = GAUSS_POINTS
    shape_values = [
        2.0 * (points - 0.5) * (points - 1.0),
        -4.0 * points * (points - 1.0),
        2.0 * points * (points - 0.5),
    ]
    shape_slopes = [4.0 * points - 3.0, 4.0 - 8.0 * points, 4.0 * points - 1.0]
    for offset in range(3):
        node_rows = (2 * np.arange(elements) + offset) % node_count
        for gauss_index in range(3):
            columns = 3 * np.arange(elements) + gauss_index
            values[node_rows, columns] += shape_values[offset][gauss_index]
            slopes[node_rows, columns] += shape_slopes[offset][gauss_index]
    return values, slopes


def round_up(value, unit):
    return -(-value // unit) * unit


def make_tables(ze, ye, xe):
    zv, zs = basis_tables(ze, False)
    yv, ys = basis_tables(ye, False)
    xv, xs = basis_tables(xe, True)
    nz, ny = zv.shape[0], yv.shape[0]
    qr, qx = 9 * ze * ye, 3 * xe
    qrp, qxp = round_up(qr, 8), round_up(qx, 128)

    def rows(tz, ty):
        out = np.zeros((qrp, nz, ROW))
        out[:qr, :, :ny] = np.einsum("zk,yl->klzy", tz, ty).reshape(qr, nz, ny)
        return out.reshape(qrp, nz * ROW)

    vv, vd, dv = rows(zv, yv), rows(zv, ys), rows(zs, yv)
    along_x = np.zeros((2 * xe, 2 * qxp))
    along_x[:, :qx] = xv
    along_x[:, qxp : qxp + qx] = xs
    weights = np.zeros((qrp, qxp))
    weights[:qr, :qx] = np.einsum(
        "z,y,x->zyx",
        np.tile(GAUSS_WEIGHTS, ze),
        np.tile(GAUSS_WEIGHTS, ye),
        np.tile(GAUSS_WEIGHTS, xe),
    ).reshape(qr, qx)
    return (
        thirds(along_x, 0),
        thirds(along_x.T, 0),
        thirds(vv, 1),
        thirds(np.concatenate([vd, dv], axis=0), 1),
        thirds(vv.T, 1),
        thirds(np.concatenate([vd.T, dv.T], axis=1), 1),
        weights.astype(np.float32),
    )


def thirds(table, axis):
    head = table.astype(ml_dtypes.bfloat16)
    tail = (table - head.astype(np.float64)).astype(ml_dtypes.bfloat16)
    return np.concatenate([head, head, tail], axis=axis)


def split(value, axis):
    head = value.astype(jnp.bfloat16).astype(jnp.float32)
    return jnp.concatenate([head, value - head, head], axis=axis).astype(jnp.bfloat16)


def dot(a, b):
    return lax.dot_general(
        a, b, (((1,), (0,)), ((), ())), preferred_element_type=jnp.float32
    )


def kernel(
    dims,
    disp_in, coef_in, elem_in, point_in, coord_in,
    xt_in, xtt_in, vv_in, vdv_in, vvt_in, vdvt_in, wts_in,
    out, lc,
    disp, coef, elem, point, coord, xt, xtt, vv, vdv, vvt, vdvt, wts,
    query, arrived, answer, found, tab, spots, scat, fld, grad,
    hy_send, hc_send, hz, hy, hc,
    ysend, csend, zrecv, yrecv, crecv, part, sums,
    l_sem, q_send, q_recv, f_send, f_recv, h_send, h_recv, x_send, x_recv, a_send, a_recv,
):
    n_mesh, n_bg, nz, ny, qx = dims
    n = n_mesh * n_bg
    cap = elem.shape[1]
    his = coef.shape[1] // LO
    qrp, qxp = wts.shape
    zi, yi = lax.axis_index("mesh"), lax.axis_index("bg")
    me = zi * n_bg + yi

    def device(index):
        return (lax.div(index, n_bg), lax.rem(index, n_bg))

    def near(dz, dy):
        return (lax.rem(zi + n_mesh + dz, n_mesh), lax.rem(yi + n_bg + dy, n_bg))

    def remote(src, dst, ssem, rsem, target):
        return pltpu.make_async_remote_copy(
            src_ref=src, dst_ref=dst, send_sem=ssem, recv_sem=rsem,
            device_id=target, device_id_type=MESH,
        )

    def wait_bytes(ref, sem):
        pltpu.make_async_copy(ref, ref, sem).wait()

    local = [
        pltpu.make_async_copy(src, dst, l_sem.at[i])
        for i, (src, dst) in enumerate(
            (
                (elem_in, elem), (coord_in, coord), (disp_in, disp), (point_in, point),
                (coef_in, coef), (xt_in, xt), (xtt_in, xtt), (vv_in, vv), (vdv_in, vdv),
                (vvt_in, vvt), (vdvt_in, vdvt), (wts_in, wts),
            )
        )
    ]
    for copy in local:
        copy.start()
    barrier = pltpu.get_barrier_semaphore()

    def greet(d, carry):
        pl.semaphore_signal(
            barrier, inc=1, device_id=device(lax.rem(me + d, n)), device_id_type=MESH
        )
        return carry

    lax.fori_loop(1, n, greet, 0)
    for copy in local[:3]:
        copy.wait()

    def pack(o, carry):
        query[o, 0:1, :] = elem[pl.ds(o, 1), :].astype(jnp.float32)
        for j in range(3):
            query[o, 1 + j : 2 + j, :] = coord[j, pl.ds(o, 1), :]
        return carry

    lax.fori_loop(0, n, pack, 0)
    for c in range(3):
        for z in range(nz - 1):
            hy_send[c, z : z + 1, :] = disp[c, z, 0:1, :]
        hc_send[c : c + 1, :] = disp[c, 0, 0:1, :]
    pl.semaphore_wait(barrier, n - 1)

    def send_query(d, carry):
        target = lax.rem(me + d, n)
        remote(
            query.at[target], arrived.at[d], q_send, q_recv.at[d], device(target)
        ).start()
        return carry

    lax.fori_loop(1, n, send_query, 0)
    halo = [
        remote(disp.at[:, 0], hz, h_send.at[0], h_recv.at[0], near(-1, 0)),
        remote(hy_send, hy, h_send.at[1], h_recv.at[1], near(0, -1)),
        remote(hc_send, hc, h_send.at[2], h_recv.at[2], near(-1, -1)),
    ]
    for copy in halo:
        copy.start()

    local[3].wait()
    qx_lanes = lax.broadcasted_iota(jnp.int32, (GROUP * cap, qxp), 1)
    places = point[...].astype(jnp.float32)
    levels = jnp.floor((places + 0.5) * (1.0 / qx))
    offsets = jnp.transpose(places - levels * qx)
    for g in range(n // GROUP):
        column = jnp.concatenate(
            [offsets[:, GROUP * g + j : GROUP * g + j + 1] for j in range(GROUP)], axis=0
        ).astype(jnp.int32)
        spots[g] = jnp.where(qx_lanes == column, 1.0, 0.0).astype(jnp.bfloat16)

    local[4].wait()
    for h in range(0, his, 2):
        pair = jnp.concatenate(
            [coef[:, LO * h : LO * (h + 1)], coef[:, LO * (h + 1) : LO * (h + 2)]], axis=0
        )
        top = pair.astype(jnp.bfloat16)
        tab[8 * h : 8 * h + 16, :LO] = top
        tab[8 * h : 8 * h + 16, LO:] = (pair - top.astype(jnp.float32)).astype(jnp.bfloat16)
    arrived[0] = query[me]

    wide = GROUP * cap
    corner = lax.broadcasted_iota(jnp.int32, (8, wide), 0)
    lo_rows = lax.broadcasted_iota(jnp.int32, (LO, wide), 0)

    def serve(g, carry):
        first = g * GROUP
        for j in range(GROUP):
            d = first + j

            @pl.when(d > 0)
            def _():
                source = device(lax.rem(me + n - d, n))
                remote(query.at[0], arrived.at[d], q_send, q_recv.at[d], source).wait_recv()

        asked = jnp.concatenate([arrived[first + j] for j in range(GROUP)], axis=1)
        ids = asked[0:1].astype(jnp.int32)
        hi = lax.shift_right_logical(ids, LO.bit_length() - 1)
        lo = lax.bitwise_and(ids, LO - 1)
        one_hot = jnp.where(lo_rows == lo, 1.0, 0.0).astype(jnp.bfloat16)
        rows = dot(tab[...], jnp.concatenate([one_hot, one_hot], axis=0))
        hi8 = jnp.broadcast_to(hi, (8, wide))
        chosen = rows[0:8]
        for h in range(1, his):
            chosen = jnp.where(hi8 == h, rows[8 * h : 8 * h + 8], chosen)
        x, y, z = (asked[j : j + 1] for j in (1, 2, 3))
        ax = jnp.where((corner & 1) != 0, x, 1.0 - x)
        ay = jnp.where((corner & 2) != 0, y, 1.0 - y)
        az = jnp.where((corner & 4) != 0, z, 1.0 - z)
        values = jnp.exp(-2.0 * jnp.sum(ax * ay * az * chosen, axis=0, keepdims=True))
        for j in range(GROUP):
            answer[first + j] = values[:, j * cap : (j + 1) * cap]
        for j in range(GROUP):
            d = first + j

            @pl.when(d > 0)
            def _():
                source = device(lax.rem(me + n - d, n))
                remote(answer.at[d], found.at[me], f_send, f_recv, source).start()

        return carry

    lax.fori_loop(0, n // GROUP, serve, 0)
    found[me] = answer[0]

    for copy in local[5:]:
        copy.wait()
    for copy in halo:
        copy.wait()
    fld[...] = jnp.zeros_like(fld)
    for c in range(3):
        for z in range(nz - 1):
            fld[c, z, 0 : ny - 1, :] = disp[c, z]
            fld[c, z, ny - 1 : ny, :] = hy[c, z : z + 1, :]
        fld[c, nz - 1, 0 : ny - 1, :] = hz[c]
        fld[c, nz - 1, ny - 1 : ny, :] = hc[c : c + 1, :]

    def derivatives(flat):
        along = dot(split(flat, 1), xt[...])
        result = []
        for c in range(3):
            rows = along[c * nz * ROW : (c + 1) * nz * ROW]
            dx = dot(vv[...], split(rows[:, qxp:], 0))
            dyz = dot(vdv[...], split(rows[:, :qxp], 0))
            result.append([dx, dyz[:qrp], dyz[qrp:]])
        return result

    jac = derivatives(fld[...].reshape(3 * nz * ROW, -1))
    for c in range(3):
        jac[c][c] = jac[c][c] + 1.0

    wait_bytes(found.at[pl.ds(0, n - 1)], f_recv)
    scat[...] = jnp.zeros_like(scat)
    hi_rows = lax.broadcasted_iota(jnp.int32, (qrp, wide), 0)

    def place(g, carry):
        first = g * GROUP
        p = jnp.concatenate([point[pl.ds(first + j, 1), :] for j in range(GROUP)], axis=1)
        level = jnp.floor((p.astype(jnp.float32) + 0.5) * (1.0 / qx)).astype(jnp.int32)
        mine = hi_rows == level
        value = jnp.concatenate([found[first + j] for j in range(GROUP)], axis=1)
        pieces = []
        for _ in range(3):
            piece = value.astype(jnp.bfloat16).astype(jnp.float32)
            value = value - piece
            pieces.append(jnp.where(mine, piece, 0.0))
        left = jnp.concatenate(pieces, axis=0).astype(jnp.bfloat16)
        scat[...] += dot(left, spots[g])
        return carry

    lax.fori_loop(0, n // GROUP, place, 0)
    scale = scat[:qrp] + scat[qrp : 2 * qrp] + scat[2 * qrp :]
    weights = wts[...]
    scale = jnp.where(weights > 0.0, scale, 0.0)

    pairs = [(k, l) for k in range(3) for l in range(k, 3)]

    def gram(a, b):
        return {
            (k, l): a[0][k] * b[0][l] + a[1][k] * b[1][l] + a[2][k] * b[2][l]
            for k, l in (pairs if a is b else [(k, l) for k in range(3) for l in range(3)])
        }

    def inner(a, b):
        diag = sum(a[k, k] * b[k, k] for k in range(3))
        off = a[0, 1] * b[0, 1] + a[0, 2] * b[0, 2] + a[1, 2] * b[1, 2]
        return jnp.sum(weights * (diag + 2.0 * off), axis=0, keepdims=True)

    for turn in range(PASSES):
        gr = gram(jac, jac)
        r0 = {kl: gr[kl] * scale - (1.0 if kl[0] == kl[1] else 0.0) for kl in pairs}
        factor = (4.0 * weights) * scale
        for c in range(3):
            pulled = []
            for k in range(3):
                total = sum(r0[min(k, l), max(k, l)] * jac[c][l] for l in range(3))
                pulled.append(total * factor)
            by_value = dot(vdvt[...], split(jnp.concatenate([pulled[1], pulled[2]], axis=0), 0))
            by_slope = dot(vvt[...], split(pulled[0], 0))
            node = dot(split(jnp.concatenate([by_value, by_slope], axis=1), 1), xtt[...])
            grad[turn, c] = node.reshape(nz, ROW, -1)

        for c in range(3):
            for side, y in enumerate((0, ny - 1)):
                for z in range(nz):
                    ysend[turn, side, c, z : z + 1, :] = grad[turn, c, z, y : y + 1, :]
                for zside, z in enumerate((0, nz - 1)):
                    csend[turn, 2 * zside + side, c : c + 1, :] = grad[turn, c, z, y : y + 1, :]
        copies = []
        for side, step in enumerate((-1, 1)):
            plane = (0, nz - 1)[side]
            copies.append((grad.at[turn, :, plane], zrecv.at[turn, 1 - side], near(step, 0)))
            copies.append((ysend.at[turn, side], yrecv.at[turn, 1 - side], near(0, step)))
            for other, ystep in enumerate((-1, 1)):
                index = 2 * side + other
                copies.append((csend.at[turn, index], crecv.at[turn, 3 - index], near(step, ystep)))
        copies = [
            remote(src, dst, x_send.at[8 * turn + i], x_recv.at[8 * turn + i], target)
            for i, (src, dst, target) in enumerate(copies)
        ]
        for copy in copies:
            copy.start()
        for copy in copies:
            copy.wait()
        for c in range(3):
            for side, z in enumerate((0, nz - 1)):
                grad[turn, c, z] += zrecv[turn, side, c]
            for side, y in enumerate((0, ny - 1)):
                for z in range(nz):
                    grad[turn, c, z, y : y + 1, :] += yrecv[turn, side, c, z : z + 1, :]
                for zside, z in enumerate((0, nz - 1)):
                    grad[turn, c, z, y : y + 1, :] += crecv[turn, 2 * zside + side, c : c + 1, :]

        direction = -grad[turn]
        move = derivatives(direction.reshape(3 * nz * ROW, -1))
        mixed = gram(jac, move)
        r1 = {(k, l): (mixed[k, l] + mixed[l, k]) * scale for k, l in pairs}
        mm = gram(move, move)
        r2 = {kl: mm[kl] * scale for kl in pairs}
        terms = [
            inner(r0, r0), inner(r0, r1), inner(r0, r2),
            inner(r1, r2), inner(r2, r2), inner(r1, r1),
        ]
        terms = jnp.concatenate(terms + [jnp.zeros((2, qxp), jnp.float32)], axis=0)
        mine = terms[:, :128]
        for lane in range(128, qxp, 128):
            mine = mine + terms[:, lane : lane + 128]
        part[turn] = mine
        sums[turn, me] = mine

        def share(d, carry, turn=turn):
            remote(
                part.at[turn], sums.at[turn, me], a_send.at[turn], a_recv.at[turn],
                device(lax.rem(me + d, n)),
            ).start()
            return carry

        lax.fori_loop(1, n, share, 0)
        wait_bytes(sums.at[turn, pl.ds(0, n - 1)], a_recv.at[turn])
        totals = jnp.sum(jnp.sum(sums[turn], axis=0), axis=1, keepdims=True)
        d00, d01, d02, d12, d22, gn = (
            jnp.broadcast_to(totals[i : i + 1], (1, 128)) for i in range(6)
        )
        c0, c1, c2, c3, c4 = d00, 2.0 * d01, gn + 2.0 * d02, 2.0 * d12, d22
        t = jnp.zeros((1, 128), jnp.float32)
        for _ in range(LS_STEPS):
            slope = c1 + t * (2.0 * c2 + t * (3.0 * c3 + t * 4.0 * c4))
            curvature = 2.0 * c2 + t * (6.0 * c3 + t * 12.0 * c4)
            t = t - slope / jnp.maximum(curvature, gn + 1e-06)
        count = n * (qrp // 9) * (qx // 3)
        for i, value in enumerate((c0, c1, c2, c3, c4)):
            lc[turn : turn + 1, i : i + 1] = value[:, :1] / count
        fld[...] = fld[...] + t.reshape(1, 1, 1, 128) * direction
        if turn + 1 < PASSES:
            step = t[:, :1]
            jac = [[jac[c][k] + step * move[c][k] for k in range(3)] for c in range(3)]

    for c in range(3):
        for z in range(nz - 1):
            out[c, z] = fld[c, z, 0 : ny - 1, :]

    wait_bytes(query.at[pl.ds(0, n - 1)], q_send)
    wait_bytes(answer.at[pl.ds(0, n - 1)], f_send)
    for turn in range(PASSES):
        wait_bytes(sums.at[turn, pl.ds(0, n - 1)], a_send.at[turn])


def shards(mesh_shape, displacement, bg_coef, query_elem, query_point, query_coord):
    n_mesh, n_bg = mesh_shape
    n = n_mesh * n_bg
    _, nz0, ny0, nx = displacement.shape
    ze, ye, xe = nz0 // 2, ny0 // 2, nx // 2
    nz, ny = nz0 + 1, ny0 + 1
    assert ny <= ROW and nx == 128
    cap = query_elem.shape[2]
    tables = make_tables(ze, ye, xe)
    qrp, qxp = tables[-1].shape
    his = bg_coef.shape[1] // LO
    f32 = jnp.float32
    dims = (n_mesh, n_bg, nz, ny, 3 * xe)
    vmem = pl.BlockSpec(memory_space=pltpu.VMEM)
    dma = pltpu.SemaphoreType.DMA
    operands = (
        displacement, bg_coef, query_elem[0], query_point[0],
        jnp.transpose(query_coord[0], (1, 0, 2)),
        *(jnp.asarray(t) for t in tables),
    )
    scratch = [
        *(pltpu.VMEM(x.shape, x.dtype) for x in operands),
        pltpu.VMEM((n, 4, cap), f32),
        pltpu.VMEM((n, 4, cap), f32),
        pltpu.VMEM((n, 1, cap), f32),
        pltpu.VMEM((n, 1, cap), f32),
        pltpu.VMEM((8 * his, 2 * LO), jnp.bfloat16),
        pltpu.VMEM((n // GROUP, GROUP * cap, qxp), jnp.bfloat16),
        pltpu.VMEM((3 * qrp, qxp), f32),
        pltpu.VMEM((3, nz, ROW, nx), f32),
        pltpu.VMEM((PASSES, 3, nz, ROW, nx), f32),
        pltpu.VMEM((3, nz0, nx), f32),
        pltpu.VMEM((3, nx), f32),
        pltpu.VMEM((3, ny0, nx), f32),
        pltpu.VMEM((3, nz0, nx), f32),
        pltpu.VMEM((3, nx), f32),
        pltpu.VMEM((PASSES, 2, 3, nz, nx), f32),
        pltpu.VMEM((PASSES, 4, 3, nx), f32),
        pltpu.VMEM((PASSES, 2, 3, ROW, nx), f32),
        pltpu.VMEM((PASSES, 2, 3, nz, nx), f32),
        pltpu.VMEM((PASSES, 4, 3, nx), f32),
        pltpu.VMEM((PASSES, 8, 128), f32),
        pltpu.VMEM((PASSES, n, 8, 128), f32),
        dma((12,)), dma, dma((n,)), dma, dma, dma((3,)), dma((3,)),
        dma((8 * PASSES,)), dma((8 * PASSES,)), dma((PASSES,)), dma((PASSES,)),
    ]
    out, lc = pl.pallas_call(
        functools.partial(kernel, dims),
        out_shape=(
            jax.ShapeDtypeStruct(displacement.shape, f32),
            jax.ShapeDtypeStruct((PASSES, 5), f32),
        ),
        in_specs=[pl.BlockSpec(memory_space=pltpu.HBM)] * 12,
        out_specs=(vmem, vmem),
        scratch_shapes=scratch,
        compiler_params=pltpu.CompilerParams(
            collective_id=0, has_side_effects=True, vmem_limit_bytes=56 * 2**20
        ),
    )(*operands)
    return out, lc


def solution(mesh):
    in_specs = (
        P(None, "mesh", "bg", None),
        P(None, ("mesh", "bg")),
        P(("mesh", "bg"), None, None),
        P(("mesh", "bg"), None, None),
        P(("mesh", "bg"), None, None, None),
    )
    out_specs = (P(None, "mesh", "bg", None), P())
    body = functools.partial(shards, (mesh.shape["mesh"], mesh.shape["bg"]))
    return jax.shard_map(body, mesh=mesh, in_specs=in_specs, out_specs=out_specs, check_vma=False)
```

```python
import functools

import jax
import jax.numpy as jnp
import ml_dtypes
import numpy as np
from jax import lax
from jax.experimental import pallas as pl
from jax.experimental.pallas import tpu as pltpu
from jax.sharding import PartitionSpec as P

PASSES = 2
LS_STEPS = 4
ROW = 8
LO = 256
GROUP = 4

GAUSS_POINTS = np.array([0.5 - 0.5 * np.sqrt(0.6), 0.5, 0.5 + 0.5 * np.sqrt(0.6)])
GAUSS_WEIGHTS = np.array([5.0 / 18.0, 8.0 / 18.0, 5.0 / 18.0])
MESH = pl.DeviceIdType.MESH


def basis_tables(elements, periodic):
    node_count = 2 * elements if periodic else 2 * elements + 1
    values = np.zeros((node_count, 3 * elements))
    slopes = np.zeros((node_count, 3 * elements))
    points = GAUSS_POINTS
    shape_values = [
        2.0 * (points - 0.5) * (points - 1.0),
        -4.0 * points * (points - 1.0),
        2.0 * points * (points - 0.5),
    ]
    shape_slopes = [4.0 * points - 3.0, 4.0 - 8.0 * points, 4.0 * points - 1.0]
    for offset in range(3):
        node_rows = (2 * np.arange(elements) + offset) % node_count
        for gauss_index in range(3):
            columns = 3 * np.arange(elements) + gauss_index
            values[node_rows, columns] += shape_values[offset][gauss_index]
            slopes[node_rows, columns] += shape_slopes[offset][gauss_index]
    return values, slopes


def round_up(value, unit):
    return -(-value // unit) * unit


def make_tables(ze, ye, xe):
    zv, zs = basis_tables(ze, False)
    yv, ys = basis_tables(ye, False)
    xv, xs = basis_tables(xe, True)
    nz, ny = zv.shape[0], yv.shape[0]
    qr, qx = 9 * ze * ye, 3 * xe
    qrp, qxp = round_up(qr, 8), round_up(qx, 128)

    def rows(tz, ty):
        out = np.zeros((qrp, nz, ROW))
        out[:qr, :, :ny] = np.einsum("zk,yl->klzy", tz, ty).reshape(qr, nz, ny)
        return out.reshape(qrp, nz * ROW)

    vv, vd, dv = rows(zv, yv), rows(zv, ys), rows(zs, yv)
    along_x = np.zeros((2 * xe, 2 * qxp))
    along_x[:, :qx] = xv
    along_x[:, qxp : qxp + qx] = xs
    weights = np.zeros((qrp, qxp))
    weights[:qr, :qx] = np.einsum(
        "z,y,x->zyx",
        np.tile(GAUSS_WEIGHTS, ze),
        np.tile(GAUSS_WEIGHTS, ye),
        np.tile(GAUSS_WEIGHTS, xe),
    ).reshape(qr, qx)
    return (
        thirds(along_x, 0),
        thirds(along_x.T, 0),
        thirds(vv, 1),
        thirds(np.concatenate([vd, dv], axis=0), 1),
        thirds(vv.T, 1),
        thirds(np.concatenate([vd.T, dv.T], axis=1), 1),
        weights.astype(np.float32),
    )


def thirds(table, axis):
    head = table.astype(ml_dtypes.bfloat16)
    tail = (table - head.astype(np.float64)).astype(ml_dtypes.bfloat16)
    return np.concatenate([head, head, tail], axis=axis)


def split(value, axis):
    head = value.astype(jnp.bfloat16).astype(jnp.float32)
    return jnp.concatenate([head, value - head, head], axis=axis).astype(jnp.bfloat16)


def dot(a, b):
    return lax.dot_general(
        a, b, (((1,), (0,)), ((), ())), preferred_element_type=jnp.float32
    )


def kernel(
    dims,
    disp_in, coef_in, elem_in, point_in, coord_in,
    xt_in, xtt_in, vv_in, vdv_in, vvt_in, vdvt_in, wts_in,
    out, lc,
    disp, coef, elem, point, coord, xt, xtt, vv, vdv, vvt, vdvt, wts,
    query, arrived, answer, found, turned, tab, spots, scat, fld, grad,
    hy_send, hc_send, hz, hy, hc,
    ysend, csend, zrecv, yrecv, crecv, part, sums,
    l_sem, q_send, q_recv, f_send, f_recv, h_send, h_recv, x_send, x_recv, a_send, a_recv,
):
    n_mesh, n_bg, nz, ny, qx = dims
    n = n_mesh * n_bg
    cap = elem.shape[1]
    his = coef.shape[1] // LO
    qrp, qxp = wts.shape
    zi, yi = lax.axis_index("mesh"), lax.axis_index("bg")
    me = zi * n_bg + yi

    def device(index):
        return (lax.div(index, n_bg), lax.rem(index, n_bg))

    def near(dz, dy):
        return (lax.rem(zi + n_mesh + dz, n_mesh), lax.rem(yi + n_bg + dy, n_bg))

    def remote(src, dst, ssem, rsem, target):
        return pltpu.make_async_remote_copy(
            src_ref=src, dst_ref=dst, send_sem=ssem, recv_sem=rsem,
            device_id=target, device_id_type=MESH,
        )

    def wait_bytes(ref, sem):
        pltpu.make_async_copy(ref, ref, sem).wait()

    local = [
        pltpu.make_async_copy(src, dst, l_sem.at[i])
        for i, (src, dst) in enumerate(
            (
                (elem_in, elem), (coord_in, coord), (disp_in, disp), (point_in, point),
                (coef_in, coef), (xt_in, xt), (xtt_in, xtt), (vv_in, vv), (vdv_in, vdv),
                (vvt_in, vvt), (vdvt_in, vdvt), (wts_in, wts),
            )
        )
    ]
    for copy in local:
        copy.start()
    barrier = pltpu.get_barrier_semaphore()

    def greet(d, carry):
        pl.semaphore_signal(
            barrier, inc=1, device_id=device(lax.rem(me + d, n)), device_id_type=MESH
        )
        return carry

    lax.fori_loop(1, n, greet, 0)
    for copy in local[:3]:
        copy.wait()

    def pack(o, carry):
        query[o, 0:1, :] = elem[pl.ds(o, 1), :].astype(jnp.float32)
        for j in range(3):
            query[o, 1 + j : 2 + j, :] = coord[j, pl.ds(o, 1), :]
        return carry

    lax.fori_loop(0, n, pack, 0)
    for c in range(3):
        for z in range(nz - 1):
            hy_send[c, z : z + 1, :] = disp[c, z, 0:1, :]
        hc_send[c : c + 1, :] = disp[c, 0, 0:1, :]
    pl.semaphore_wait(barrier, n - 1)

    def send_query(d, carry):
        target = lax.rem(me + d, n)
        remote(
            query.at[target], arrived.at[d], q_send, q_recv.at[d], device(target)
        ).start()
        return carry

    lax.fori_loop(1, n, send_query, 0)
    halo = [
        remote(disp.at[:, 0], hz, h_send.at[0], h_recv.at[0], near(-1, 0)),
        remote(hy_send, hy, h_send.at[1], h_recv.at[1], near(0, -1)),
        remote(hc_send, hc, h_send.at[2], h_recv.at[2], near(-1, -1)),
    ]
    for copy in halo:
        copy.start()

    local[3].wait()
    qx_lanes = lax.broadcasted_iota(jnp.int32, (GROUP * cap, qxp), 1)

    def turn_rows(d, carry):
        turned[pl.ds(d, 1), :] = point[pl.ds(lax.rem(me + d, n), 1), :].astype(jnp.float32)
        return carry

    lax.fori_loop(0, n, turn_rows, 0)
    places = turned[...]
    offsets = jnp.transpose(places - jnp.floor((places + 0.5) * (1.0 / qx)) * qx)
    for g in range(n // GROUP):
        column = jnp.concatenate(
            [offsets[:, GROUP * g + j : GROUP * g + j + 1] for j in range(GROUP)], axis=0
        ).astype(jnp.int32)
        spots[g] = jnp.where(qx_lanes == column, 1.0, 0.0).astype(jnp.bfloat16)

    local[4].wait()
    for h in range(0, his, 2):
        pair = jnp.concatenate(
            [coef[:, LO * h : LO * (h + 1)], coef[:, LO * (h + 1) : LO * (h + 2)]], axis=0
        )
        top = pair.astype(jnp.bfloat16)
        tab[8 * h : 8 * h + 16, :LO] = top
        tab[8 * h : 8 * h + 16, LO:] = (pair - top.astype(jnp.float32)).astype(jnp.bfloat16)
    arrived[0] = query[me]

    wide = GROUP * cap
    corner = lax.broadcasted_iota(jnp.int32, (8, wide), 0)
    lo_rows = lax.broadcasted_iota(jnp.int32, (LO, wide), 0)

    hi_rows = lax.broadcasted_iota(jnp.int32, (qrp, wide), 0)

    def source(d):
        return device(lax.rem(me + n - d, n))

    def await_queries(g):
        for j in range(GROUP):
            d = g * GROUP + j

            @pl.when(d > 0)
            def _():
                remote(query.at[0], arrived.at[d], q_send, q_recv.at[d], source(d)).wait_recv()

    def await_answers(g):
        for j in range(GROUP):
            d = g * GROUP + j

            @pl.when(d > 0)
            def _():
                remote(answer.at[0], found.at[d], f_send, f_recv.at[d], source(d)).wait_recv()

    def reply(g):
        for j in range(GROUP):
            d = g * GROUP + j

            @pl.when(d > 0)
            def _():
                remote(answer.at[d], found.at[d], f_send, f_recv.at[d], source(d)).start()

            if j == 0:

                @pl.when(d == 0)
                def _():
                    found[0] = answer[0]

    def serve(g):
        first = g * GROUP
        asked = jnp.concatenate([arrived[first + j] for j in range(GROUP)], axis=1)
        ids = asked[0:1].astype(jnp.int32)
        hi = lax.shift_right_logical(ids, LO.bit_length() - 1)
        lo = lax.bitwise_and(ids, LO - 1)
        one_hot = jnp.where(lo_rows == lo, 1.0, 0.0).astype(jnp.bfloat16)
        rows = dot(tab[...], jnp.concatenate([one_hot, one_hot], axis=0))
        hi8 = jnp.broadcast_to(hi, (8, wide))
        chosen = rows[0:8]
        for h in range(1, his):
            chosen = jnp.where(hi8 == h, rows[8 * h : 8 * h + 8], chosen)
        x, y, z = (asked[j : j + 1] for j in (1, 2, 3))
        ax = jnp.where((corner & 1) != 0, x, 1.0 - x)
        ay = jnp.where((corner & 2) != 0, y, 1.0 - y)
        az = jnp.where((corner & 4) != 0, z, 1.0 - z)
        values = jnp.exp(-2.0 * jnp.sum(ax * ay * az * chosen, axis=0, keepdims=True))
        for j in range(GROUP):
            answer[first + j] = values[:, j * cap : (j + 1) * cap]

    def place(g):
        first = g * GROUP
        p = jnp.concatenate([turned[pl.ds(first + j, 1), :] for j in range(GROUP)], axis=1)
        level = jnp.floor((p + 0.5) * (1.0 / qx)).astype(jnp.int32)
        mine = hi_rows == level
        value = jnp.concatenate([found[first + j] for j in range(GROUP)], axis=1)
        pieces = []
        for _ in range(3):
            piece = value.astype(jnp.bfloat16).astype(jnp.float32)
            value = value - piece
            pieces.append(jnp.where(mine, piece, 0.0))
        left = jnp.concatenate(pieces, axis=0).astype(jnp.bfloat16)
        scat[...] += dot(left, spots[g])

    def only_serve(g, carry):
        await_queries(g)
        serve(g)
        reply(g)
        return carry

    def serve_and_place(g, carry):
        await_queries(g)
        await_answers(g - 2)
        serve(g)
        place(g - 2)
        reply(g)
        return carry

    def only_place(g, carry):
        await_answers(g)
        place(g)
        return carry

    groups = n // GROUP
    scat[...] = jnp.zeros_like(scat)
    lax.fori_loop(0, 2, only_serve, 0)
    lax.fori_loop(2, groups, serve_and_place, 0)

    for copy in local[5:]:
        copy.wait()
    for copy in halo:
        copy.wait()
    fld[...] = jnp.zeros_like(fld)
    for c in range(3):
        for z in range(nz - 1):
            fld[c, z, 0 : ny - 1, :] = disp[c, z]
            fld[c, z, ny - 1 : ny, :] = hy[c, z : z + 1, :]
        fld[c, nz - 1, 0 : ny - 1, :] = hz[c]
        fld[c, nz - 1, ny - 1 : ny, :] = hc[c : c + 1, :]

    def derivatives(flat):
        along = dot(split(flat, 1), xt[...])
        result = []
        for c in range(3):
            rows = along[c * nz * ROW : (c + 1) * nz * ROW]
            dx = dot(vv[...], split(rows[:, qxp:], 0))
            dyz = dot(vdv[...], split(rows[:, :qxp], 0))
            result.append([dx, dyz[:qrp], dyz[qrp:]])
        return result

    jac = derivatives(fld[...].reshape(3 * nz * ROW, -1))
    for c in range(3):
        jac[c][c] = jac[c][c] + 1.0

    lax.fori_loop(groups - 2, groups, only_place, 0)
    scale = scat[:qrp] + scat[qrp : 2 * qrp] + scat[2 * qrp :]
    weights = wts[...]
    scale = jnp.where(weights > 0.0, scale, 0.0)

    pairs = [(k, l) for k in range(3) for l in range(k, 3)]

    def gram(a, b):
        return {
            (k, l): a[0][k] * b[0][l] + a[1][k] * b[1][l] + a[2][k] * b[2][l]
            for k, l in (pairs if a is b else [(k, l) for k in range(3) for l in range(3)])
        }

    def inner(a, b):
        diag = sum(a[k, k] * b[k, k] for k in range(3))
        off = a[0, 1] * b[0, 1] + a[0, 2] * b[0, 2] + a[1, 2] * b[1, 2]
        return jnp.sum(weights * (diag + 2.0 * off), axis=0, keepdims=True)

    for turn in range(PASSES):
        gr = gram(jac, jac)
        r0 = {kl: gr[kl] * scale - (1.0 if kl[0] == kl[1] else 0.0) for kl in pairs}
        factor = (4.0 * weights) * scale
        across = []
        for c in range(3):
            pulled = []
            for k in range(3):
                total = sum(r0[min(k, l), max(k, l)] * jac[c][l] for l in range(3))
                pulled.append(total * factor)
            by_value = dot(vdvt[...], split(jnp.concatenate([pulled[1], pulled[2]], axis=0), 0))
            by_slope = dot(vvt[...], split(pulled[0], 0))
            across.append(jnp.concatenate([by_value, by_slope], axis=1))
        node = dot(split(jnp.concatenate(across, axis=0), 1), xtt[...])
        grad[turn] = node.reshape(3, nz, ROW, -1)

        for c in range(3):
            for side, y in enumerate((0, ny - 1)):
                for z in range(nz):
                    ysend[turn, side, c, z : z + 1, :] = grad[turn, c, z, y : y + 1, :]
                for zside, z in enumerate((0, nz - 1)):
                    csend[turn, 2 * zside + side, c : c + 1, :] = grad[turn, c, z, y : y + 1, :]
        copies = []
        for side, step in enumerate((-1, 1)):
            plane = (0, nz - 1)[side]
            copies.append((grad.at[turn, :, plane], zrecv.at[turn, 1 - side], near(step, 0)))
            copies.append((ysend.at[turn, side], yrecv.at[turn, 1 - side], near(0, step)))
            for other, ystep in enumerate((-1, 1)):
                index = 2 * side + other
                copies.append((csend.at[turn, index], crecv.at[turn, 3 - index], near(step, ystep)))
        copies = [
            remote(src, dst, x_send.at[8 * turn + i], x_recv.at[8 * turn + i], target)
            for i, (src, dst, target) in enumerate(copies)
        ]
        for copy in copies:
            copy.start()
        for copy in copies:
            copy.wait()
        for c in range(3):
            for side, z in enumerate((0, nz - 1)):
                grad[turn, c, z] += zrecv[turn, side, c]
            for side, y in enumerate((0, ny - 1)):
                for z in range(nz):
                    grad[turn, c, z, y : y + 1, :] += yrecv[turn, side, c, z : z + 1, :]
                for zside, z in enumerate((0, nz - 1)):
                    grad[turn, c, z, y : y + 1, :] += crecv[turn, 2 * zside + side, c : c + 1, :]

        direction = -grad[turn]
        move = derivatives(direction.reshape(3 * nz * ROW, -1))
        mixed = gram(jac, move)
        r1 = {(k, l): (mixed[k, l] + mixed[l, k]) * scale for k, l in pairs}
        mm = gram(move, move)
        r2 = {kl: mm[kl] * scale for kl in pairs}
        terms = [
            inner(r0, r0), inner(r0, r1), inner(r0, r2),
            inner(r1, r2), inner(r2, r2), inner(r1, r1),
        ]
        terms = jnp.concatenate(terms + [jnp.zeros((2, qxp), jnp.float32)], axis=0)
        mine = terms[:, :128]
        for lane in range(128, qxp, 128):
            mine = mine + terms[:, lane : lane + 128]
        part[turn] = mine
        sums[turn, me] = mine

        def share(d, carry, turn=turn):
            remote(
                part.at[turn], sums.at[turn, me], a_send.at[turn], a_recv.at[turn],
                device(lax.rem(me + d, n)),
            ).start()
            return carry

        lax.fori_loop(1, n, share, 0)
        wait_bytes(sums.at[turn, pl.ds(0, n - 1)], a_recv.at[turn])
        totals = jnp.sum(jnp.sum(sums[turn], axis=0), axis=1, keepdims=True)
        d00, d01, d02, d12, d22, gn = (
            jnp.broadcast_to(totals[i : i + 1], (1, 128)) for i in range(6)
        )
        c0, c1, c2, c3, c4 = d00, 2.0 * d01, gn + 2.0 * d02, 2.0 * d12, d22
        t = jnp.zeros((1, 128), jnp.float32)
        for _ in range(LS_STEPS):
            slope = c1 + t * (2.0 * c2 + t * (3.0 * c3 + t * 4.0 * c4))
            curvature = 2.0 * c2 + t * (6.0 * c3 + t * 12.0 * c4)
            t = t - slope / jnp.maximum(curvature, gn + 1e-06)
        count = n * (qrp // 9) * (qx // 3)
        for i, value in enumerate((c0, c1, c2, c3, c4)):
            lc[turn : turn + 1, i : i + 1] = value[:, :1] / count
        fld[...] = fld[...] + t.reshape(1, 1, 1, 128) * direction
        if turn + 1 < PASSES:
            step = t[:, :1]
            jac = [[jac[c][k] + step * move[c][k] for k in range(3)] for c in range(3)]

    for c in range(3):
        for z in range(nz - 1):
            out[c, z] = fld[c, z, 0 : ny - 1, :]

    wait_bytes(query.at[pl.ds(0, n - 1)], q_send)
    wait_bytes(answer.at[pl.ds(0, n - 1)], f_send)
    for turn in range(PASSES):
        wait_bytes(sums.at[turn, pl.ds(0, n - 1)], a_send.at[turn])


def shards(mesh_shape, displacement, bg_coef, query_elem, query_point, query_coord):
    n_mesh, n_bg = mesh_shape
    n = n_mesh * n_bg
    _, nz0, ny0, nx = displacement.shape
    ze, ye, xe = nz0 // 2, ny0 // 2, nx // 2
    nz, ny = nz0 + 1, ny0 + 1
    assert ny <= ROW and nx == 128
    cap = query_elem.shape[2]
    tables = make_tables(ze, ye, xe)
    qrp, qxp = tables[-1].shape
    his = bg_coef.shape[1] // LO
    f32 = jnp.float32
    dims = (n_mesh, n_bg, nz, ny, 3 * xe)
    vmem = pl.BlockSpec(memory_space=pltpu.VMEM)
    dma = pltpu.SemaphoreType.DMA
    operands = (
        displacement, bg_coef, query_elem[0], query_point[0],
        jnp.transpose(query_coord[0], (1, 0, 2)),
        *(jnp.asarray(t) for t in tables),
    )
    scratch = [
        *(pltpu.VMEM(x.shape, x.dtype) for x in operands),
        pltpu.VMEM((n, 4, cap), f32),
        pltpu.VMEM((n, 4, cap), f32),
        pltpu.VMEM((n, 1, cap), f32),
        pltpu.VMEM((n, 1, cap), f32),
        pltpu.VMEM((n, cap), f32),
        pltpu.VMEM((8 * his, 2 * LO), jnp.bfloat16),
        pltpu.VMEM((n // GROUP, GROUP * cap, qxp), jnp.bfloat16),
        pltpu.VMEM((3 * qrp, qxp), f32),
        pltpu.VMEM((3, nz, ROW, nx), f32),
        pltpu.VMEM((PASSES, 3, nz, ROW, nx), f32),
        pltpu.VMEM((3, nz0, nx), f32),
        pltpu.VMEM((3, nx), f32),
        pltpu.VMEM((3, ny0, nx), f32),
        pltpu.VMEM((3, nz0, nx), f32),
        pltpu.VMEM((3, nx), f32),
        pltpu.VMEM((PASSES, 2, 3, nz, nx), f32),
        pltpu.VMEM((PASSES, 4, 3, nx), f32),
        pltpu.VMEM((PASSES, 2, 3, ROW, nx), f32),
        pltpu.VMEM((PASSES, 2, 3, nz, nx), f32),
        pltpu.VMEM((PASSES, 4, 3, nx), f32),
        pltpu.VMEM((PASSES, 8, 128), f32),
        pltpu.VMEM((PASSES, n, 8, 128), f32),
        dma((12,)), dma, dma((n,)), dma, dma((n,)), dma((3,)), dma((3,)),
        dma((8 * PASSES,)), dma((8 * PASSES,)), dma((PASSES,)), dma((PASSES,)),
    ]
    out, lc = pl.pallas_call(
        functools.partial(kernel, dims),
        out_shape=(
            jax.ShapeDtypeStruct(displacement.shape, f32),
            jax.ShapeDtypeStruct((PASSES, 5), f32),
        ),
        in_specs=[pl.BlockSpec(memory_space=pltpu.HBM)] * 12,
        out_specs=(vmem, vmem),
        scratch_shapes=scratch,
        compiler_params=pltpu.CompilerParams(
            collective_id=0, has_side_effects=True, vmem_limit_bytes=56 * 2**20
        ),
    )(*operands)
    return out, lc


def solution(mesh):
    in_specs = (
        P(None, "mesh", "bg", None),
        P(None, ("mesh", "bg")),
        P(("mesh", "bg"), None, None),
        P(("mesh", "bg"), None, None),
        P(("mesh", "bg"), None, None, None),
    )
    out_specs = (P(None, "mesh", "bg", None), P())
    body = functools.partial(shards, (mesh.shape["mesh"], mesh.shape["bg"]))
    return jax.shard_map(body, mesh=mesh, in_specs=in_specs, out_specs=out_specs, check_vma=False)
```

```python
import functools

import jax
import jax.numpy as jnp
import ml_dtypes
import numpy as np
from jax import lax
from jax.experimental import pallas as pl
from jax.experimental.pallas import tpu as pltpu
from jax.sharding import PartitionSpec as P

PASSES = 2
LS_STEPS = 4
ROW = 8
LO = 256

GAUSS_POINTS = np.array([0.5 - 0.5 * np.sqrt(0.6), 0.5, 0.5 + 0.5 * np.sqrt(0.6)])
GAUSS_WEIGHTS = np.array([5.0 / 18.0, 8.0 / 18.0, 5.0 / 18.0])
MESH = pl.DeviceIdType.MESH


def basis_tables(elements, periodic):
    node_count = 2 * elements if periodic else 2 * elements + 1
    values = np.zeros((node_count, 3 * elements))
    slopes = np.zeros((node_count, 3 * elements))
    points = GAUSS_POINTS
    shape_values = [
        2.0 * (points - 0.5) * (points - 1.0),
        -4.0 * points * (points - 1.0),
        2.0 * points * (points - 0.5),
    ]
    shape_slopes = [4.0 * points - 3.0, 4.0 - 8.0 * points, 4.0 * points - 1.0]
    for offset in range(3):
        node_rows = (2 * np.arange(elements) + offset) % node_count
        for gauss_index in range(3):
            columns = 3 * np.arange(elements) + gauss_index
            values[node_rows, columns] += shape_values[offset][gauss_index]
            slopes[node_rows, columns] += shape_slopes[offset][gauss_index]
    return values, slopes


def round_up(value, unit):
    return -(-value // unit) * unit


def make_tables(ze, ye, xe):
    zv, zs = basis_tables(ze, False)
    yv, ys = basis_tables(ye, False)
    xv, xs = basis_tables(xe, True)
    nz, ny = zv.shape[0], yv.shape[0]
    qr, qx = 9 * ze * ye, 3 * xe
    qrp, qxp = round_up(qr, 8), round_up(qx, 128)

    def rows(tz, ty):
        out = np.zeros((qrp, nz, ROW))
        out[:qr, :, :ny] = np.einsum("zk,yl->klzy", tz, ty).reshape(qr, nz, ny)
        return out.reshape(qrp, nz * ROW)

    vv, vd, dv = rows(zv, yv), rows(zv, ys), rows(zs, yv)
    along_x = np.zeros((2 * xe, 2 * qxp))
    along_x[:, :qx] = xv
    along_x[:, qxp : qxp + qx] = xs
    weights = np.zeros((qrp, qxp))
    weights[:qr, :qx] = np.einsum(
        "z,y,x->zyx",
        np.tile(GAUSS_WEIGHTS, ze),
        np.tile(GAUSS_WEIGHTS, ye),
        np.tile(GAUSS_WEIGHTS, xe),
    ).reshape(qr, qx)
    return (
        thirds(along_x, 0),
        thirds(along_x.T, 0),
        thirds(vv, 1),
        thirds(np.concatenate([vd, dv], axis=0), 1),
        thirds(vv.T, 1),
        thirds(np.concatenate([vd.T, dv.T], axis=1), 1),
        weights.astype(np.float32),
    )


def thirds(table, axis):
    head = table.astype(ml_dtypes.bfloat16)
    tail = (table - head.astype(np.float64)).astype(ml_dtypes.bfloat16)
    return np.concatenate([head, head, tail], axis=axis)


def split(value, axis):
    head = value.astype(jnp.bfloat16).astype(jnp.float32)
    return jnp.concatenate([head, value - head, head], axis=axis).astype(jnp.bfloat16)


def dot(a, b):
    return lax.dot_general(
        a, b, (((1,), (0,)), ((), ())), preferred_element_type=jnp.float32
    )


def kernel(
    dims,
    disp_in, coef_in, elem_in, point_in, coord_in,
    xt_in, xtt_in, vv_in, vdv_in, vvt_in, vdvt_in, wts_in,
    out, lc,
    disp, coef, elem, point, coord, xt, xtt, vv, vdv, vvt, vdvt, wts,
    query, arrived, answer, found, tab, spots, scat, fld, grad,
    hy_send, hc_send, hz, hy, hc,
    ysend, csend, zrecv, yrecv, crecv, part, sums,
    l_sem, q_send, q_recv, f_send, f_recv, h_send, h_recv, x_send, x_recv, a_send, a_recv,
):
    n_mesh, n_bg, nz, ny, qx = dims
    n = n_mesh * n_bg
    cap = elem.shape[1]
    his = coef.shape[1] // LO
    qrp, qxp = wts.shape
    zi, yi = lax.axis_index("mesh"), lax.axis_index("bg")
    me = zi * n_bg + yi

    group = n_bg
    ahead = [lax.rem(yi + dy, n_bg) for dy in range(n_bg)]
    behind = [lax.rem(yi + (n_bg - dy), n_bg) for dy in range(n_bg)]

    def each_partner(act):
        for dy in range(1, n_bg):
            act(dy, zi * n_bg + ahead[dy], (zi, ahead[dy]))

        def row(dz, carry):
            z = lax.rem(zi + dz, n_mesh)
            for dy in range(n_bg):
                act(dz * n_bg + dy, z * n_bg + ahead[dy], (z, ahead[dy]))
            return carry

        lax.fori_loop(1, n_mesh, row, 0)

    def near(dz, dy):
        return (lax.rem(zi + n_mesh + dz, n_mesh), lax.rem(yi + n_bg + dy, n_bg))

    def remote(src, dst, ssem, rsem, target):
        return pltpu.make_async_remote_copy(
            src_ref=src, dst_ref=dst, send_sem=ssem, recv_sem=rsem,
            device_id=target, device_id_type=MESH,
        )

    def wait_bytes(ref, sem):
        pltpu.make_async_copy(ref, ref, sem).wait()

    local = [
        pltpu.make_async_copy(src, dst, l_sem.at[i])
        for i, (src, dst) in enumerate(
            (
                (elem_in, elem), (coord_in, coord), (disp_in, disp), (point_in, point),
                (coef_in, coef), (xt_in, xt), (xtt_in, xtt), (vv_in, vv), (vdv_in, vdv),
                (vvt_in, vvt), (vdvt_in, vdvt), (wts_in, wts),
            )
        )
    ]
    for copy in local:
        copy.start()
    barrier = pltpu.get_barrier_semaphore()

    def greet(slot, index, target):
        pl.semaphore_signal(barrier, inc=1, device_id=target, device_id_type=MESH)

    each_partner(greet)
    for copy in local[:3]:
        copy.wait()

    def pack(o, carry):
        query[o, 0:1, :] = elem[pl.ds(o, 1), :].astype(jnp.float32)
        for j in range(3):
            query[o, 1 + j : 2 + j, :] = coord[j, pl.ds(o, 1), :]
        return carry

    lax.fori_loop(0, n, pack, 0)
    for c in range(3):
        for z in range(nz - 1):
            hy_send[c, z : z + 1, :] = disp[c, z, 0:1, :]
        hc_send[c : c + 1, :] = disp[c, 0, 0:1, :]
    pl.semaphore_wait(barrier, n - 1)

    def send_query(slot, index, target):
        remote(query.at[index], arrived.at[slot], q_send, q_recv.at[slot], target).start()

    each_partner(send_query)
    halo = [
        remote(disp.at[:, 0], hz, h_send.at[0], h_recv.at[0], near(-1, 0)),
        remote(hy_send, hy, h_send.at[1], h_recv.at[1], near(0, -1)),
        remote(hc_send, hc, h_send.at[2], h_recv.at[2], near(-1, -1)),
    ]
    for copy in halo:
        copy.start()

    local[3].wait()
    one, zero = jnp.bfloat16(1.0), jnp.bfloat16(0.0)
    qx_lanes = lax.broadcasted_iota(jnp.int32, (group * cap, qxp), 1).astype(jnp.bfloat16)
    places = point[...].astype(jnp.float32)
    levels = jnp.floor((places + 0.5) * (1.0 / qx))
    offsets = jnp.transpose(places - levels * qx)
    for g in range(n // group):
        column = jnp.concatenate(
            [offsets[:, group * g + j : group * g + j + 1] for j in range(group)], axis=0
        ).astype(jnp.bfloat16)
        spots[g] = jnp.where(qx_lanes == column, one, zero)

    local[4].wait()
    for h in range(0, his, 2):
        pair = jnp.concatenate(
            [coef[:, LO * h : LO * (h + 1)], coef[:, LO * (h + 1) : LO * (h + 2)]], axis=0
        )
        top = pair.astype(jnp.bfloat16)
        tab[8 * h : 8 * h + 16, :LO] = top
        tab[8 * h : 8 * h + 16, LO:] = (pair - top.astype(jnp.float32)).astype(jnp.bfloat16)
    arrived[0] = query[me]

    wide = group * cap
    corner = lax.broadcasted_iota(jnp.int32, (8, wide), 0)
    lo_rows = lax.broadcasted_iota(jnp.int32, (LO, wide), 0).astype(jnp.bfloat16)

    def serve(g, carry):
        first = g * group
        back = lax.rem(zi + (n_mesh - g), n_mesh)

        def await_query(j):
            d = first + j
            remote(
                query.at[0], arrived.at[d], q_send, q_recv.at[d], (back, behind[j])
            ).wait_recv()

        def reply(j):
            remote(
                answer.at[first + j], found.at[me], f_send, f_recv, (back, behind[j])
            ).start()

        for j in range(1, group):
            await_query(j)
        pl.when(g > 0)(functools.partial(await_query, 0))

        asked = jnp.concatenate([arrived[first + j] for j in range(group)], axis=1)
        ids = asked[0:1].astype(jnp.int32)
        hi = lax.shift_right_logical(ids, LO.bit_length() - 1)
        lo = lax.bitwise_and(ids, LO - 1).astype(jnp.float32).astype(jnp.bfloat16)
        one_hot = jnp.where(lo_rows == lo, one, zero)
        rows = dot(tab[...], jnp.concatenate([one_hot, one_hot], axis=0))
        hi8 = jnp.broadcast_to(hi, (8, wide))
        chosen = rows[0:8]
        for h in range(1, his):
            chosen = jnp.where(hi8 == h, rows[8 * h : 8 * h + 8], chosen)
        x, y, z = (asked[j : j + 1] for j in (1, 2, 3))
        ax = jnp.where((corner & 1) != 0, x, 1.0 - x)
        ay = jnp.where((corner & 2) != 0, y, 1.0 - y)
        az = jnp.where((corner & 4) != 0, z, 1.0 - z)
        values = jnp.exp(-2.0 * jnp.sum(ax * ay * az * chosen, axis=0, keepdims=True))
        for j in range(group):
            answer[first + j] = values[:, j * cap : (j + 1) * cap]
        for j in range(1, group):
            reply(j)
        pl.when(g > 0)(functools.partial(reply, 0))
        return carry

    lax.fori_loop(0, n // group, serve, 0)
    found[me] = answer[0]

    for copy in local[5:]:
        copy.wait()
    for copy in halo:
        copy.wait()
    fld[...] = jnp.zeros_like(fld)
    for c in range(3):
        for z in range(nz - 1):
            fld[c, z, 0 : ny - 1, :] = disp[c, z]
            fld[c, z, ny - 1 : ny, :] = hy[c, z : z + 1, :]
        fld[c, nz - 1, 0 : ny - 1, :] = hz[c]
        fld[c, nz - 1, ny - 1 : ny, :] = hc[c : c + 1, :]

    def derivatives(flat):
        along = dot(split(flat, 1), xt[...])
        result = []
        for c in range(3):
            rows = along[c * nz * ROW : (c + 1) * nz * ROW]
            dx = dot(vv[...], split(rows[:, qxp:], 0))
            dyz = dot(vdv[...], split(rows[:, :qxp], 0))
            result.append([dx, dyz[:qrp], dyz[qrp:]])
        return result

    jac = derivatives(fld[...].reshape(3 * nz * ROW, -1))
    for c in range(3):
        jac[c][c] = jac[c][c] + 1.0

    wait_bytes(found.at[pl.ds(0, n - 1)], f_recv)
    scat[...] = jnp.zeros_like(scat)
    hi_rows = lax.broadcasted_iota(jnp.int32, (qrp, wide), 0)

    def place(g, carry):
        first = g * group
        p = jnp.concatenate([point[pl.ds(first + j, 1), :] for j in range(group)], axis=1)
        level = jnp.floor((p.astype(jnp.float32) + 0.5) * (1.0 / qx)).astype(jnp.int32)
        mine = hi_rows == level
        value = jnp.concatenate([found[first + j] for j in range(group)], axis=1)
        pieces = []
        for _ in range(3):
            piece = value.astype(jnp.bfloat16).astype(jnp.float32)
            value = value - piece
            pieces.append(jnp.where(mine, piece, 0.0))
        left = jnp.concatenate(pieces, axis=0).astype(jnp.bfloat16)
        scat[...] += dot(left, spots[g])
        return carry

    lax.fori_loop(0, n // group, place, 0)
    scale = scat[:qrp] + scat[qrp : 2 * qrp] + scat[2 * qrp :]
    weights = wts[...]
    scale = jnp.where(weights > 0.0, scale, 0.0)

    pairs = [(k, l) for k in range(3) for l in range(k, 3)]

    def gram(a, b):
        return {
            (k, l): a[0][k] * b[0][l] + a[1][k] * b[1][l] + a[2][k] * b[2][l]
            for k, l in (pairs if a is b else [(k, l) for k in range(3) for l in range(3)])
        }

    def inner(a, b):
        diag = sum(a[k, k] * b[k, k] for k in range(3))
        off = a[0, 1] * b[0, 1] + a[0, 2] * b[0, 2] + a[1, 2] * b[1, 2]
        return jnp.sum(weights * (diag + 2.0 * off), axis=0, keepdims=True)

    for turn in range(PASSES):
        gr = gram(jac, jac)
        r0 = {kl: gr[kl] * scale - (1.0 if kl[0] == kl[1] else 0.0) for kl in pairs}
        factor = (4.0 * weights) * scale
        across = []
        for c in range(3):
            pulled = []
            for k in range(3):
                total = sum(r0[min(k, l), max(k, l)] * jac[c][l] for l in range(3))
                pulled.append(total * factor)
            by_value = dot(vdvt[...], split(jnp.concatenate([pulled[1], pulled[2]], axis=0), 0))
            by_slope = dot(vvt[...], split(pulled[0], 0))
            across.append(jnp.concatenate([by_value, by_slope], axis=1))
        node = dot(split(jnp.concatenate(across, axis=0), 1), xtt[...])
        grad[turn] = node.reshape(3, nz, ROW, -1)

        for c in range(3):
            for side, y in enumerate((0, ny - 1)):
                for z in range(nz):
                    ysend[turn, side, c, z : z + 1, :] = grad[turn, c, z, y : y + 1, :]
                for zside, z in enumerate((0, nz - 1)):
                    csend[turn, 2 * zside + side, c : c + 1, :] = grad[turn, c, z, y : y + 1, :]
        copies = []
        for side, step in enumerate((-1, 1)):
            plane = (0, nz - 1)[side]
            copies.append((grad.at[turn, :, plane], zrecv.at[turn, 1 - side], near(step, 0)))
            copies.append((ysend.at[turn, side], yrecv.at[turn, 1 - side], near(0, step)))
            for other, ystep in enumerate((-1, 1)):
                index = 2 * side + other
                copies.append((csend.at[turn, index], crecv.at[turn, 3 - index], near(step, ystep)))
        copies = [
            remote(src, dst, x_send.at[8 * turn + i], x_recv.at[8 * turn + i], target)
            for i, (src, dst, target) in enumerate(copies)
        ]
        for copy in copies:
            copy.start()
        for copy in copies:
            copy.wait()
        for c in range(3):
            for side, z in enumerate((0, nz - 1)):
                grad[turn, c, z] += zrecv[turn, side, c]
            for side, y in enumerate((0, ny - 1)):
                for z in range(nz):
                    grad[turn, c, z, y : y + 1, :] += yrecv[turn, side, c, z : z + 1, :]
                for zside, z in enumerate((0, nz - 1)):
                    grad[turn, c, z, y : y + 1, :] += crecv[turn, 2 * zside + side, c : c + 1, :]

        direction = -grad[turn]
        move = derivatives(direction.reshape(3 * nz * ROW, -1))
        mixed = gram(jac, move)
        r1 = {(k, l): (mixed[k, l] + mixed[l, k]) * scale for k, l in pairs}
        mm = gram(move, move)
        r2 = {kl: mm[kl] * scale for kl in pairs}
        terms = [
            inner(r0, r0), inner(r0, r1), inner(r0, r2),
            inner(r1, r2), inner(r2, r2), inner(r1, r1),
        ]
        terms = jnp.concatenate(terms + [jnp.zeros((2, qxp), jnp.float32)], axis=0)
        mine = terms[:, :128]
        for lane in range(128, qxp, 128):
            mine = mine + terms[:, lane : lane + 128]
        part[turn] = mine
        sums[turn, me] = mine

        def share(slot, index, target, turn=turn):
            remote(
                part.at[turn], sums.at[turn, me], a_send.at[turn], a_recv.at[turn], target
            ).start()

        each_partner(share)
        wait_bytes(sums.at[turn, pl.ds(0, n - 1)], a_recv.at[turn])
        totals = jnp.sum(jnp.sum(sums[turn], axis=0), axis=1, keepdims=True)
        d00, d01, d02, d12, d22, gn = (
            jnp.broadcast_to(totals[i : i + 1], (1, 128)) for i in range(6)
        )
        c0, c1, c2, c3, c4 = d00, 2.0 * d01, gn + 2.0 * d02, 2.0 * d12, d22
        t = jnp.zeros((1, 128), jnp.float32)
        for _ in range(LS_STEPS):
            slope = c1 + t * (2.0 * c2 + t * (3.0 * c3 + t * 4.0 * c4))
            curvature = 2.0 * c2 + t * (6.0 * c3 + t * 12.0 * c4)
            t = t - slope / jnp.maximum(curvature, gn + 1e-06)
        count = n * (qrp // 9) * (qx // 3)
        for i, value in enumerate((c0, c1, c2, c3, c4)):
            lc[turn : turn + 1, i : i + 1] = value[:, :1] / count
        fld[...] = fld[...] + t.reshape(1, 1, 1, 128) * direction
        if turn + 1 < PASSES:
            step = t[:, :1]
            jac = [[jac[c][k] + step * move[c][k] for k in range(3)] for c in range(3)]

    for c in range(3):
        for z in range(nz - 1):
            at = (c * (nz - 1) + z) * (ny - 1)
            out[at : at + ny - 1, :] = fld[c, z, 0 : ny - 1, :]

    wait_bytes(query.at[pl.ds(0, n - 1)], q_send)
    wait_bytes(answer.at[pl.ds(0, n - 1)], f_send)
    for turn in range(PASSES):
        wait_bytes(sums.at[turn, pl.ds(0, n - 1)], a_send.at[turn])


def shards(mesh_shape, displacement, bg_coef, query_elem, query_point, query_coord):
    n_mesh, n_bg = mesh_shape
    n = n_mesh * n_bg
    _, nz0, ny0, nx = displacement.shape
    ze, ye, xe = nz0 // 2, ny0 // 2, nx // 2
    nz, ny = nz0 + 1, ny0 + 1
    assert ny <= ROW and nx == 128
    cap = query_elem.shape[2]
    tables = make_tables(ze, ye, xe)
    qrp, qxp = tables[-1].shape
    his = bg_coef.shape[1] // LO
    f32 = jnp.float32
    dims = (n_mesh, n_bg, nz, ny, 3 * xe)
    vmem = pl.BlockSpec(memory_space=pltpu.VMEM)
    dma = pltpu.SemaphoreType.DMA
    operands = (
        displacement, bg_coef, query_elem[0], query_point[0],
        jnp.transpose(query_coord[0], (1, 0, 2)),
        *(jnp.asarray(t) for t in tables),
    )
    scratch = [
        *(pltpu.VMEM(x.shape, x.dtype) for x in operands),
        pltpu.VMEM((n, 4, cap), f32),
        pltpu.VMEM((n, 4, cap), f32),
        pltpu.VMEM((n, 1, cap), f32),
        pltpu.VMEM((n, 1, cap), f32),
        pltpu.VMEM((8 * his, 2 * LO), jnp.bfloat16),
        pltpu.VMEM((n_mesh, n_bg * cap, qxp), jnp.bfloat16),
        pltpu.VMEM((3 * qrp, qxp), f32),
        pltpu.VMEM((3, nz, ROW, nx), f32),
        pltpu.VMEM((PASSES, 3, nz, ROW, nx), f32),
        pltpu.VMEM((3, nz0, nx), f32),
        pltpu.VMEM((3, nx), f32),
        pltpu.VMEM((3, ny0, nx), f32),
        pltpu.VMEM((3, nz0, nx), f32),
        pltpu.VMEM((3, nx), f32),
        pltpu.VMEM((PASSES, 2, 3, nz, nx), f32),
        pltpu.VMEM((PASSES, 4, 3, nx), f32),
        pltpu.VMEM((PASSES, 2, 3, ROW, nx), f32),
        pltpu.VMEM((PASSES, 2, 3, nz, nx), f32),
        pltpu.VMEM((PASSES, 4, 3, nx), f32),
        pltpu.VMEM((PASSES, 8, 128), f32),
        pltpu.VMEM((PASSES, n, 8, 128), f32),
        dma((12,)), dma, dma((n,)), dma, dma, dma((3,)), dma((3,)),
        dma((8 * PASSES,)), dma((8 * PASSES,)), dma((PASSES,)), dma((PASSES,)),
    ]
    out, lc = pl.pallas_call(
        functools.partial(kernel, dims),
        out_shape=(
            jax.ShapeDtypeStruct((3 * nz0 * ny0, nx), f32),
            jax.ShapeDtypeStruct((PASSES, 5), f32),
        ),
        in_specs=[pl.BlockSpec(memory_space=pltpu.HBM)] * 12,
        out_specs=(vmem, vmem),
        scratch_shapes=scratch,
        compiler_params=pltpu.CompilerParams(
            collective_id=0, has_side_effects=True, vmem_limit_bytes=56 * 2**20
        ),
    )(*operands)
    return out.reshape(displacement.shape), lc


def solution(mesh):
    in_specs = (
        P(None, "mesh", "bg", None),
        P(None, ("mesh", "bg")),
        P(("mesh", "bg"), None, None),
        P(("mesh", "bg"), None, None),
        P(("mesh", "bg"), None, None, None),
    )
    out_specs = (P(None, "mesh", "bg", None), P())
    body = functools.partial(shards, (mesh.shape["mesh"], mesh.shape["bg"]))
    return jax.shard_map(body, mesh=mesh, in_specs=in_specs, out_specs=out_specs, check_vma=False)
```

```python
import functools

import jax
import jax.numpy as jnp
import ml_dtypes
import numpy as np
from jax import lax
from jax.experimental import pallas as pl
from jax.experimental.pallas import tpu as pltpu
from jax.sharding import PartitionSpec as P

PASSES = 2
LS_STEPS = 4
ROW = 8
LO = 256
CHUNK = 768

GAUSS_POINTS = np.array([0.5 - 0.5 * np.sqrt(0.6), 0.5, 0.5 + 0.5 * np.sqrt(0.6)])
GAUSS_WEIGHTS = np.array([5.0 / 18.0, 8.0 / 18.0, 5.0 / 18.0])
MESH = pl.DeviceIdType.MESH


def basis_tables(elements, periodic):
    node_count = 2 * elements if periodic else 2 * elements + 1
    values = np.zeros((node_count, 3 * elements))
    slopes = np.zeros((node_count, 3 * elements))
    points = GAUSS_POINTS
    shape_values = [
        2.0 * (points - 0.5) * (points - 1.0),
        -4.0 * points * (points - 1.0),
        2.0 * points * (points - 0.5),
    ]
    shape_slopes = [4.0 * points - 3.0, 4.0 - 8.0 * points, 4.0 * points - 1.0]
    for offset in range(3):
        node_rows = (2 * np.arange(elements) + offset) % node_count
        for gauss_index in range(3):
            columns = 3 * np.arange(elements) + gauss_index
            values[node_rows, columns] += shape_values[offset][gauss_index]
            slopes[node_rows, columns] += shape_slopes[offset][gauss_index]
    return values, slopes


def round_up(value, unit):
    return -(-value // unit) * unit


def make_tables(ze, ye, xe):
    zv, zs = basis_tables(ze, False)
    yv, ys = basis_tables(ye, False)
    xv, xs = basis_tables(xe, True)
    nz, ny = zv.shape[0], yv.shape[0]
    qr, qx = 9 * ze * ye, 3 * xe
    qrp, qxp = round_up(qr, 8), round_up(qx, 128)

    def rows(tz, ty):
        out = np.zeros((qrp, nz, ROW))
        out[:qr, :, :ny] = np.einsum("zk,yl->klzy", tz, ty).reshape(qr, nz, ny)
        return out.reshape(qrp, nz * ROW)

    vv, vd, dv = rows(zv, yv), rows(zv, ys), rows(zs, yv)
    along_x = np.zeros((2 * xe, 2 * qxp))
    along_x[:, :qx] = xv
    along_x[:, qxp : qxp + qx] = xs
    weights = np.zeros((qrp, qxp))
    weights[:qr, :qx] = np.einsum(
        "z,y,x->zyx",
        np.tile(GAUSS_WEIGHTS, ze),
        np.tile(GAUSS_WEIGHTS, ye),
        np.tile(GAUSS_WEIGHTS, xe),
    ).reshape(qr, qx)
    return (
        thirds(along_x, 0),
        thirds(along_x.T, 0),
        thirds(vv, 1),
        thirds(np.concatenate([vd, dv], axis=0), 1),
        thirds(vv.T, 1),
        thirds(np.concatenate([vd.T, dv.T], axis=1), 1),
        weights.astype(np.float32),
    )


def thirds(table, axis):
    head = table.astype(ml_dtypes.bfloat16)
    tail = (table - head.astype(np.float64)).astype(ml_dtypes.bfloat16)
    return np.concatenate([head, head, tail], axis=axis)


def split(value, axis):
    head = value.astype(jnp.bfloat16).astype(jnp.float32)
    return jnp.concatenate([head, value - head, head], axis=axis).astype(jnp.bfloat16)


def dot(a, b):
    return lax.dot_general(
        a, b, (((1,), (0,)), ((), ())), preferred_element_type=jnp.float32
    )


def kernel(
    dims,
    disp_in, coef_in, elem_in, point_in, coord_in,
    xt_in, xtt_in, vv_in, vdv_in, vvt_in, vdvt_in, wts_in,
    out, lc,
    disp, coef, elem, point, coord, xt, xtt, vv, vdv, vvt, vdvt, wts,
    query, arrived, answer, found, tab, spots, scat, fld, grad,
    hy_send, hc_send, hz, hy, hc,
    ysend, csend, zrecv, yrecv, crecv, part, sums,
    l_sem, q_send, q_recv, f_send, f_recv, h_send, h_recv, x_send, x_recv, a_send, a_recv,
):
    n_mesh, n_bg, nz, ny, qx = dims
    n = n_mesh * n_bg
    cap = elem.shape[1]
    his = coef.shape[1] // LO
    qrp, qxp = wts.shape
    zi, yi = lax.axis_index("mesh"), lax.axis_index("bg")
    me = zi * n_bg + yi

    group = n_bg
    ahead = [lax.rem(yi + dy, n_bg) for dy in range(n_bg)]
    behind = [lax.rem(yi + (n_bg - dy), n_bg) for dy in range(n_bg)]

    def each_partner(act):
        for dy in range(1, n_bg):
            act(dy, zi * n_bg + ahead[dy], (zi, ahead[dy]))

        def row(dz, carry):
            z = lax.rem(zi + dz, n_mesh)
            for dy in range(n_bg):
                act(dz * n_bg + dy, z * n_bg + ahead[dy], (z, ahead[dy]))
            return carry

        lax.fori_loop(1, n_mesh, row, 0)

    def near(dz, dy):
        return (lax.rem(zi + n_mesh + dz, n_mesh), lax.rem(yi + n_bg + dy, n_bg))

    def remote(src, dst, ssem, rsem, target):
        return pltpu.make_async_remote_copy(
            src_ref=src, dst_ref=dst, send_sem=ssem, recv_sem=rsem,
            device_id=target, device_id_type=MESH,
        )

    def wait_bytes(ref, sem):
        pltpu.make_async_copy(ref, ref, sem).wait()

    local = [
        pltpu.make_async_copy(src, dst, l_sem.at[i])
        for i, (src, dst) in enumerate(
            (
                (elem_in, elem), (coord_in, coord), (disp_in, disp), (point_in, point),
                (coef_in, coef), (xt_in, xt), (xtt_in, xtt), (vv_in, vv), (vdv_in, vdv),
                (vvt_in, vvt), (vdvt_in, vdvt), (wts_in, wts),
            )
        )
    ]
    for copy in local:
        copy.start()
    barrier = pltpu.get_barrier_semaphore()

    def greet(slot, index, target):
        pl.semaphore_signal(barrier, inc=1, device_id=target, device_id_type=MESH)

    each_partner(greet)
    for copy in local[:3]:
        copy.wait()

    def pack(o, carry):
        query[o, 0:1, :] = elem[pl.ds(o, 1), :].astype(jnp.float32)
        for j in range(3):
            query[o, 1 + j : 2 + j, :] = coord[j, pl.ds(o, 1), :]
        return carry

    lax.fori_loop(0, n, pack, 0)
    for c in range(3):
        for z in range(nz - 1):
            hy_send[c, z : z + 1, :] = disp[c, z, 0:1, :]
        hc_send[c : c + 1, :] = disp[c, 0, 0:1, :]
    pl.semaphore_wait(barrier, n - 1)

    def send_query(slot, index, target):
        remote(query.at[index], arrived.at[slot], q_send, q_recv.at[slot], target).start()

    each_partner(send_query)
    halo = [
        remote(disp.at[:, 0], hz, h_send.at[0], h_recv.at[0], near(-1, 0)),
        remote(hy_send, hy, h_send.at[1], h_recv.at[1], near(0, -1)),
        remote(hc_send, hc, h_send.at[2], h_recv.at[2], near(-1, -1)),
    ]
    for copy in halo:
        copy.start()

    local[3].wait()
    one, zero = jnp.bfloat16(1.0), jnp.bfloat16(0.0)
    qx_lanes = lax.broadcasted_iota(jnp.int32, (group * cap, qxp), 1).astype(jnp.bfloat16)
    places = point[...].astype(jnp.float32)
    levels = jnp.floor((places + 0.5) * (1.0 / qx))
    offsets = jnp.transpose(places - levels * qx)
    for g in range(n // group):
        column = jnp.concatenate(
            [offsets[:, group * g + j : group * g + j + 1] for j in range(group)], axis=0
        ).astype(jnp.bfloat16)
        spots[g] = jnp.where(qx_lanes == column, one, zero)

    local[4].wait()
    for h in range(0, his, 2):
        pair = jnp.concatenate(
            [coef[:, LO * h : LO * (h + 1)], coef[:, LO * (h + 1) : LO * (h + 2)]], axis=0
        )
        top = pair.astype(jnp.bfloat16)
        tab[8 * h : 8 * h + 16, :LO] = top
        tab[8 * h : 8 * h + 16, LO:] = (pair - top.astype(jnp.float32)).astype(jnp.bfloat16)
    arrived[0] = query[me]

    wide = group * cap
    corner = lax.broadcasted_iota(jnp.int32, (8, wide), 0)
    lo_rows = lax.broadcasted_iota(jnp.int32, (LO, wide), 0).astype(jnp.bfloat16)

    def serve(g, carry):
        first = g * group
        back = lax.rem(zi + (n_mesh - g), n_mesh)

        def await_query(j):
            d = first + j
            remote(
                query.at[0], arrived.at[d], q_send, q_recv.at[d], (back, behind[j])
            ).wait_recv()

        def reply(j):
            remote(
                answer.at[first + j], found.at[me], f_send, f_recv, (back, behind[j])
            ).start()

        for j in range(1, group):
            await_query(j)
        pl.when(g > 0)(functools.partial(await_query, 0))

        asked = jnp.concatenate([arrived[first + j] for j in range(group)], axis=1)
        ids = asked[0:1].astype(jnp.int32)
        hi = lax.shift_right_logical(ids, LO.bit_length() - 1)
        lo = lax.bitwise_and(ids, LO - 1).astype(jnp.float32).astype(jnp.bfloat16)
        picked = []
        for at in range(0, wide, CHUNK):
            end = min(at + CHUNK, wide)
            one_hot = jnp.where(lo_rows[:, at:end] == lo[:, at:end], one, zero)
            rows = dot(tab[...], jnp.concatenate([one_hot, one_hot], axis=0))
            hi8 = jnp.broadcast_to(hi[:, at:end], (8, end - at))
            chosen = rows[0:8]
            for h in range(1, his):
                chosen = jnp.where(hi8 == h, rows[8 * h : 8 * h + 8], chosen)
            picked.append(chosen)
        chosen = jnp.concatenate(picked, axis=1)
        x, y, z = (asked[j : j + 1] for j in (1, 2, 3))
        ax = jnp.where((corner & 1) != 0, x, 1.0 - x)
        ay = jnp.where((corner & 2) != 0, y, 1.0 - y)
        az = jnp.where((corner & 4) != 0, z, 1.0 - z)
        values = jnp.exp(-2.0 * jnp.sum(ax * ay * az * chosen, axis=0, keepdims=True))
        for j in range(group):
            answer[first + j] = values[:, j * cap : (j + 1) * cap]
        for j in range(1, group):
            reply(j)
        pl.when(g > 0)(functools.partial(reply, 0))
        return carry

    lax.fori_loop(0, n // group, serve, 0)
    found[me] = answer[0]

    for copy in local[5:]:
        copy.wait()
    for copy in halo:
        copy.wait()
    fld[...] = jnp.zeros_like(fld)
    for c in range(3):
        for z in range(nz - 1):
            fld[c, z, 0 : ny - 1, :] = disp[c, z]
            fld[c, z, ny - 1 : ny, :] = hy[c, z : z + 1, :]
        fld[c, nz - 1, 0 : ny - 1, :] = hz[c]
        fld[c, nz - 1, ny - 1 : ny, :] = hc[c : c + 1, :]

    def derivatives(flat):
        along = dot(split(flat, 1), xt[...])
        result = []
        for c in range(3):
            rows = along[c * nz * ROW : (c + 1) * nz * ROW]
            dx = dot(vv[...], split(rows[:, qxp:], 0))
            dyz = dot(vdv[...], split(rows[:, :qxp], 0))
            result.append([dx, dyz[:qrp], dyz[qrp:]])
        return result

    jac = derivatives(fld[...].reshape(3 * nz * ROW, -1))
    for c in range(3):
        jac[c][c] = jac[c][c] + 1.0

    wait_bytes(found.at[pl.ds(0, n - 1)], f_recv)
    scat[...] = jnp.zeros_like(scat)
    hi_rows = lax.broadcasted_iota(jnp.int32, (qrp, wide), 0)

    def place(g, carry):
        first = g * group
        p = jnp.concatenate([point[pl.ds(first + j, 1), :] for j in range(group)], axis=1)
        level = jnp.floor((p.astype(jnp.float32) + 0.5) * (1.0 / qx)).astype(jnp.int32)
        mine = hi_rows == level
        value = jnp.concatenate([found[first + j] for j in range(group)], axis=1)
        pieces = []
        for _ in range(3):
            piece = value.astype(jnp.bfloat16).astype(jnp.float32)
            value = value - piece
            pieces.append(jnp.where(mine, piece, 0.0))
        left = jnp.concatenate(pieces, axis=0).astype(jnp.bfloat16)
        scat[...] += dot(left, spots[g])
        return carry

    lax.fori_loop(0, n // group, place, 0)
    scale = scat[:qrp] + scat[qrp : 2 * qrp] + scat[2 * qrp :]
    weights = wts[...]
    scale = jnp.where(weights > 0.0, scale, 0.0)

    pairs = [(k, l) for k in range(3) for l in range(k, 3)]

    def gram(a, b):
        return {
            (k, l): a[0][k] * b[0][l] + a[1][k] * b[1][l] + a[2][k] * b[2][l]
            for k, l in (pairs if a is b else [(k, l) for k in range(3) for l in range(3)])
        }

    def inner(a, b):
        diag = sum(a[k, k] * b[k, k] for k in range(3))
        off = a[0, 1] * b[0, 1] + a[0, 2] * b[0, 2] + a[1, 2] * b[1, 2]
        return jnp.sum(weights * (diag + 2.0 * off), axis=0, keepdims=True)

    for turn in range(PASSES):
        gr = gram(jac, jac)
        r0 = {kl: gr[kl] * scale - (1.0 if kl[0] == kl[1] else 0.0) for kl in pairs}
        factor = (4.0 * weights) * scale
        across = []
        for c in range(3):
            pulled = []
            for k in range(3):
                total = sum(r0[min(k, l), max(k, l)] * jac[c][l] for l in range(3))
                pulled.append(total * factor)
            by_value = dot(vdvt[...], split(jnp.concatenate([pulled[1], pulled[2]], axis=0), 0))
            by_slope = dot(vvt[...], split(pulled[0], 0))
            across.append(jnp.concatenate([by_value, by_slope], axis=1))
        node = dot(split(jnp.concatenate(across, axis=0), 1), xtt[...])
        grad[turn] = node.reshape(3, nz, ROW, -1)

        for c in range(3):
            for side, y in enumerate((0, ny - 1)):
                for z in range(nz):
                    ysend[turn, side, c, z : z + 1, :] = grad[turn, c, z, y : y + 1, :]
                for zside, z in enumerate((0, nz - 1)):
                    csend[turn, 2 * zside + side, c : c + 1, :] = grad[turn, c, z, y : y + 1, :]
        copies = []
        for side, step in enumerate((-1, 1)):
            plane = (0, nz - 1)[side]
            copies.append((grad.at[turn, :, plane], zrecv.at[turn, 1 - side], near(step, 0)))
            copies.append((ysend.at[turn, side], yrecv.at[turn, 1 - side], near(0, step)))
            for other, ystep in enumerate((-1, 1)):
                index = 2 * side + other
                copies.append((csend.at[turn, index], crecv.at[turn, 3 - index], near(step, ystep)))
        copies = [
            remote(src, dst, x_send.at[8 * turn + i], x_recv.at[8 * turn + i], target)
            for i, (src, dst, target) in enumerate(copies)
        ]
        for copy in copies:
            copy.start()
        for copy in copies:
            copy.wait()
        for c in range(3):
            for side, z in enumerate((0, nz - 1)):
                grad[turn, c, z] += zrecv[turn, side, c]
            for side, y in enumerate((0, ny - 1)):
                for z in range(nz):
                    grad[turn, c, z, y : y + 1, :] += yrecv[turn, side, c, z : z + 1, :]
                for zside, z in enumerate((0, nz - 1)):
                    grad[turn, c, z, y : y + 1, :] += crecv[turn, 2 * zside + side, c : c + 1, :]

        direction = -grad[turn]
        move = derivatives(direction.reshape(3 * nz * ROW, -1))
        mixed = gram(jac, move)
        r1 = {(k, l): (mixed[k, l] + mixed[l, k]) * scale for k, l in pairs}
        mm = gram(move, move)
        r2 = {kl: mm[kl] * scale for kl in pairs}
        terms = [
            inner(r0, r0), inner(r0, r1), inner(r0, r2),
            inner(r1, r2), inner(r2, r2), inner(r1, r1),
        ]
        terms = jnp.concatenate(terms + [jnp.zeros((2, qxp), jnp.float32)], axis=0)
        mine = terms[:, :128]
        for lane in range(128, qxp, 128):
            mine = mine + terms[:, lane : lane + 128]
        part[turn] = mine
        sums[turn, me] = mine

        def share(slot, index, target, turn=turn):
            remote(
                part.at[turn], sums.at[turn, me], a_send.at[turn], a_recv.at[turn], target
            ).start()

        each_partner(share)
        wait_bytes(sums.at[turn, pl.ds(0, n - 1)], a_recv.at[turn])
        totals = jnp.sum(jnp.sum(sums[turn], axis=0), axis=1, keepdims=True)
        d00, d01, d02, d12, d22, gn = (
            jnp.broadcast_to(totals[i : i + 1], (1, 128)) for i in range(6)
        )
        c0, c1, c2, c3, c4 = d00, 2.0 * d01, gn + 2.0 * d02, 2.0 * d12, d22
        t = jnp.zeros((1, 128), jnp.float32)
        for _ in range(LS_STEPS):
            slope = c1 + t * (2.0 * c2 + t * (3.0 * c3 + t * 4.0 * c4))
            curvature = 2.0 * c2 + t * (6.0 * c3 + t * 12.0 * c4)
            t = t - slope / jnp.maximum(curvature, gn + 1e-06)
        count = n * (qrp // 9) * (qx // 3)
        for i, value in enumerate((c0, c1, c2, c3, c4)):
            lc[turn : turn + 1, i : i + 1] = value[:, :1] / count
        fld[...] = fld[...] + t.reshape(1, 1, 1, 128) * direction
        if turn + 1 < PASSES:
            step = t[:, :1]
            jac = [[jac[c][k] + step * move[c][k] for k in range(3)] for c in range(3)]

    for c in range(3):
        for z in range(nz - 1):
            at = (c * (nz - 1) + z) * (ny - 1)
            out[at : at + ny - 1, :] = fld[c, z, 0 : ny - 1, :]

    wait_bytes(query.at[pl.ds(0, n - 1)], q_send)
    wait_bytes(answer.at[pl.ds(0, n - 1)], f_send)
    for turn in range(PASSES):
        wait_bytes(sums.at[turn, pl.ds(0, n - 1)], a_send.at[turn])


def shards(mesh_shape, displacement, bg_coef, query_elem, query_point, query_coord):
    n_mesh, n_bg = mesh_shape
    n = n_mesh * n_bg
    _, nz0, ny0, nx = displacement.shape
    ze, ye, xe = nz0 // 2, ny0 // 2, nx // 2
    nz, ny = nz0 + 1, ny0 + 1
    assert ny <= ROW and nx == 128
    cap = query_elem.shape[2]
    tables = make_tables(ze, ye, xe)
    qrp, qxp = tables[-1].shape
    his = bg_coef.shape[1] // LO
    f32 = jnp.float32
    dims = (n_mesh, n_bg, nz, ny, 3 * xe)
    vmem = pl.BlockSpec(memory_space=pltpu.VMEM)
    dma = pltpu.SemaphoreType.DMA
    operands = (
        displacement, bg_coef, query_elem[0], query_point[0],
        jnp.transpose(query_coord[0], (1, 0, 2)),
        *(jnp.asarray(t) for t in tables),
    )
    scratch = [
        *(pltpu.VMEM(x.shape, x.dtype) for x in operands),
        pltpu.VMEM((n, 4, cap), f32),
        pltpu.VMEM((n, 4, cap), f32),
        pltpu.VMEM((n, 1, cap), f32),
        pltpu.VMEM((n, 1, cap), f32),
        pltpu.VMEM((8 * his, 2 * LO), jnp.bfloat16),
        pltpu.VMEM((n_mesh, n_bg * cap, qxp), jnp.bfloat16),
        pltpu.VMEM((3 * qrp, qxp), f32),
        pltpu.VMEM((3, nz, ROW, nx), f32),
        pltpu.VMEM((PASSES, 3, nz, ROW, nx), f32),
        pltpu.VMEM((3, nz0, nx), f32),
        pltpu.VMEM((3, nx), f32),
        pltpu.VMEM((3, ny0, nx), f32),
        pltpu.VMEM((3, nz0, nx), f32),
        pltpu.VMEM((3, nx), f32),
        pltpu.VMEM((PASSES, 2, 3, nz, nx), f32),
        pltpu.VMEM((PASSES, 4, 3, nx), f32),
        pltpu.VMEM((PASSES, 2, 3, ROW, nx), f32),
        pltpu.VMEM((PASSES, 2, 3, nz, nx), f32),
        pltpu.VMEM((PASSES, 4, 3, nx), f32),
        pltpu.VMEM((PASSES, 8, 128), f32),
        pltpu.VMEM((PASSES, n, 8, 128), f32),
        dma((12,)), dma, dma((n,)), dma, dma, dma((3,)), dma((3,)),
        dma((8 * PASSES,)), dma((8 * PASSES,)), dma((PASSES,)), dma((PASSES,)),
    ]
    out, lc = pl.pallas_call(
        functools.partial(kernel, dims),
        out_shape=(
            jax.ShapeDtypeStruct((3 * nz0 * ny0, nx), f32),
            jax.ShapeDtypeStruct((PASSES, 5), f32),
        ),
        in_specs=[pl.BlockSpec(memory_space=pltpu.HBM)] * 12,
        out_specs=(vmem, vmem),
        scratch_shapes=scratch,
        compiler_params=pltpu.CompilerParams(
            collective_id=0, has_side_effects=True, vmem_limit_bytes=56 * 2**20
        ),
    )(*operands)
    return out.reshape(displacement.shape), lc


def solution(mesh):
    in_specs = (
        P(None, "mesh", "bg", None),
        P(None, ("mesh", "bg")),
        P(("mesh", "bg"), None, None),
        P(("mesh", "bg"), None, None),
        P(("mesh", "bg"), None, None, None),
    )
    out_specs = (P(None, "mesh", "bg", None), P())
    body = functools.partial(shards, (mesh.shape["mesh"], mesh.shape["bg"]))
    return jax.shard_map(body, mesh=mesh, in_specs=in_specs, out_specs=out_specs, check_vma=False)
```

```python
import functools

import jax
import jax.numpy as jnp
import ml_dtypes
import numpy as np
from jax import lax
from jax.experimental import pallas as pl
from jax.experimental.pallas import tpu as pltpu
from jax.sharding import PartitionSpec as P

PASSES = 2
LS_STEPS = 4
ROW = 8
LO = 128
CHUNK = 768

GAUSS_POINTS = np.array([0.5 - 0.5 * np.sqrt(0.6), 0.5, 0.5 + 0.5 * np.sqrt(0.6)])
GAUSS_WEIGHTS = np.array([5.0 / 18.0, 8.0 / 18.0, 5.0 / 18.0])
MESH = pl.DeviceIdType.MESH


def basis_tables(elements, periodic):
    node_count = 2 * elements if periodic else 2 * elements + 1
    values = np.zeros((node_count, 3 * elements))
    slopes = np.zeros((node_count, 3 * elements))
    points = GAUSS_POINTS
    shape_values = [
        2.0 * (points - 0.5) * (points - 1.0),
        -4.0 * points * (points - 1.0),
        2.0 * points * (points - 0.5),
    ]
    shape_slopes = [4.0 * points - 3.0, 4.0 - 8.0 * points, 4.0 * points - 1.0]
    for offset in range(3):
        node_rows = (2 * np.arange(elements) + offset) % node_count
        for gauss_index in range(3):
            columns = 3 * np.arange(elements) + gauss_index
            values[node_rows, columns] += shape_values[offset][gauss_index]
            slopes[node_rows, columns] += shape_slopes[offset][gauss_index]
    return values, slopes


def round_up(value, unit):
    return -(-value // unit) * unit


def make_tables(ze, ye, xe):
    zv, zs = basis_tables(ze, False)
    yv, ys = basis_tables(ye, False)
    xv, xs = basis_tables(xe, True)
    nz, ny = zv.shape[0], yv.shape[0]
    qr, qx = 9 * ze * ye, 3 * xe
    qrp, qxp = round_up(qr, 8), round_up(qx, 128)

    def rows(tz, ty):
        out = np.zeros((qrp, nz, ROW))
        out[:qr, :, :ny] = np.einsum("zk,yl->klzy", tz, ty).reshape(qr, nz, ny)
        return out.reshape(qrp, nz * ROW)

    vv, vd, dv = rows(zv, yv), rows(zv, ys), rows(zs, yv)
    along_x = np.zeros((2 * xe, 2 * qxp))
    along_x[:, :qx] = xv
    along_x[:, qxp : qxp + qx] = xs
    weights = np.zeros((qrp, qxp))
    weights[:qr, :qx] = np.einsum(
        "z,y,x->zyx",
        np.tile(GAUSS_WEIGHTS, ze),
        np.tile(GAUSS_WEIGHTS, ye),
        np.tile(GAUSS_WEIGHTS, xe),
    ).reshape(qr, qx)
    return (
        thirds(along_x, 0),
        thirds(along_x.T, 0),
        thirds(vv, 1),
        thirds(np.concatenate([vd, dv], axis=0), 1),
        thirds(vv.T, 1),
        thirds(np.concatenate([vd.T, dv.T], axis=1), 1),
        weights.astype(np.float32),
    )


def thirds(table, axis):
    head = table.astype(ml_dtypes.bfloat16)
    tail = (table - head.astype(np.float64)).astype(ml_dtypes.bfloat16)
    return np.concatenate([head, head, tail], axis=axis)


def split(value, axis):
    head = value.astype(jnp.bfloat16).astype(jnp.float32)
    return jnp.concatenate([head, value - head, head], axis=axis).astype(jnp.bfloat16)


def dot(a, b):
    return lax.dot_general(
        a, b, (((1,), (0,)), ((), ())), preferred_element_type=jnp.float32
    )


def kernel(
    dims,
    disp_in, coef_in, elem_in, point_in, coord_in,
    xt_in, xtt_in, vv_in, vdv_in, vvt_in, vdvt_in, wts_in,
    out, lc,
    disp, coef, elem, point, coord, xt, xtt, vv, vdv, vvt, vdvt, wts,
    query, arrived, answer, found, tab, spots, scat, fld, grad,
    hy_send, hc_send, hz, hy, hc,
    ysend, csend, zrecv, yrecv, crecv, part, sums,
    l_sem, q_send, q_recv, f_send, f_recv, h_send, h_recv, x_send, x_recv, a_send, a_recv,
):
    n_mesh, n_bg, nz, ny, qx = dims
    n = n_mesh * n_bg
    cap = elem.shape[1]
    his = coef.shape[1] // LO
    qrp, qxp = wts.shape
    zi, yi = lax.axis_index("mesh"), lax.axis_index("bg")
    me = zi * n_bg + yi

    group = n_bg
    ahead = [lax.rem(yi + dy, n_bg) for dy in range(n_bg)]
    behind = [lax.rem(yi + (n_bg - dy), n_bg) for dy in range(n_bg)]

    def each_partner(act):
        for dy in range(1, n_bg):
            act(dy, zi * n_bg + ahead[dy], (zi, ahead[dy]))

        def row(dz, carry):
            z = lax.rem(zi + dz, n_mesh)
            for dy in range(n_bg):
                act(dz * n_bg + dy, z * n_bg + ahead[dy], (z, ahead[dy]))
            return carry

        lax.fori_loop(1, n_mesh, row, 0)

    def near(dz, dy):
        return (lax.rem(zi + n_mesh + dz, n_mesh), lax.rem(yi + n_bg + dy, n_bg))

    def remote(src, dst, ssem, rsem, target):
        return pltpu.make_async_remote_copy(
            src_ref=src, dst_ref=dst, send_sem=ssem, recv_sem=rsem,
            device_id=target, device_id_type=MESH,
        )

    def wait_bytes(ref, sem):
        pltpu.make_async_copy(ref, ref, sem).wait()

    local = [
        pltpu.make_async_copy(src, dst, l_sem.at[i])
        for i, (src, dst) in enumerate(
            (
                (elem_in, elem), (coord_in, coord), (disp_in, disp), (point_in, point),
                (coef_in, coef), (xt_in, xt), (xtt_in, xtt), (vv_in, vv), (vdv_in, vdv),
                (vvt_in, vvt), (vdvt_in, vdvt), (wts_in, wts),
            )
        )
    ]
    for copy in local:
        copy.start()
    barrier = pltpu.get_barrier_semaphore()

    def greet(slot, index, target):
        pl.semaphore_signal(barrier, inc=1, device_id=target, device_id_type=MESH)

    each_partner(greet)
    for copy in local[:3]:
        copy.wait()

    def pack(o, carry):
        query[o, 0:1, :] = elem[pl.ds(o, 1), :].astype(jnp.float32)
        for j in range(3):
            query[o, 1 + j : 2 + j, :] = coord[j, pl.ds(o, 1), :]
        return carry

    lax.fori_loop(0, n, pack, 0)
    for c in range(3):
        for z in range(nz - 1):
            hy_send[c, z : z + 1, :] = disp[c, z, 0:1, :]
        hc_send[c : c + 1, :] = disp[c, 0, 0:1, :]
    pl.semaphore_wait(barrier, n - 1)

    def send_query(slot, index, target):
        remote(query.at[index], arrived.at[slot], q_send, q_recv.at[slot], target).start()

    each_partner(send_query)
    halo = [
        remote(disp.at[:, 0], hz, h_send.at[0], h_recv.at[0], near(-1, 0)),
        remote(hy_send, hy, h_send.at[1], h_recv.at[1], near(0, -1)),
        remote(hc_send, hc, h_send.at[2], h_recv.at[2], near(-1, -1)),
    ]
    for copy in halo:
        copy.start()

    local[3].wait()
    one, zero = jnp.bfloat16(1.0), jnp.bfloat16(0.0)
    qx_lanes = lax.broadcasted_iota(jnp.int32, (group * cap, qxp), 1).astype(jnp.bfloat16)
    places = point[...].astype(jnp.float32)
    levels = jnp.floor((places + 0.5) * (1.0 / qx))
    offsets = jnp.transpose(places - levels * qx)
    for g in range(n // group):
        column = jnp.concatenate(
            [offsets[:, group * g + j : group * g + j + 1] for j in range(group)], axis=0
        ).astype(jnp.bfloat16)
        spots[g] = jnp.where(qx_lanes == column, one, zero)

    local[4].wait()
    for h in range(0, his, 2):
        pair = jnp.concatenate(
            [coef[:, LO * h : LO * (h + 1)], coef[:, LO * (h + 1) : LO * (h + 2)]], axis=0
        )
        top = pair.astype(jnp.bfloat16)
        tab[8 * h : 8 * h + 16, :LO] = top
        tab[8 * h : 8 * h + 16, LO:] = (pair - top.astype(jnp.float32)).astype(jnp.bfloat16)
    arrived[0] = query[me]

    wide = group * cap
    corner = lax.broadcasted_iota(jnp.int32, (8, wide), 0)
    lo_rows = lax.broadcasted_iota(jnp.int32, (LO, wide), 0).astype(jnp.bfloat16)

    def serve(g, carry):
        first = g * group
        back = lax.rem(zi + (n_mesh - g), n_mesh)

        def await_query(j):
            d = first + j
            remote(
                query.at[0], arrived.at[d], q_send, q_recv.at[d], (back, behind[j])
            ).wait_recv()

        def reply(j):
            remote(
                answer.at[first + j], found.at[me], f_send, f_recv, (back, behind[j])
            ).start()

        for j in range(1, group):
            await_query(j)
        pl.when(g > 0)(functools.partial(await_query, 0))

        asked = jnp.concatenate([arrived[first + j] for j in range(group)], axis=1)
        ids = asked[0:1].astype(jnp.int32)
        hi = lax.shift_right_logical(ids, LO.bit_length() - 1)
        lo = lax.bitwise_and(ids, LO - 1).astype(jnp.float32).astype(jnp.bfloat16)
        picked = []
        for at in range(0, wide, CHUNK):
            end = min(at + CHUNK, wide)
            one_hot = jnp.where(lo_rows[:, at:end] == lo[:, at:end], one, zero)
            rows = dot(tab[...], jnp.concatenate([one_hot, one_hot], axis=0))
            hi8 = jnp.broadcast_to(hi[:, at:end], (8, end - at))
            chosen = rows[0:8]
            for h in range(1, his):
                chosen = jnp.where(hi8 == h, rows[8 * h : 8 * h + 8], chosen)
            picked.append(chosen)
        chosen = jnp.concatenate(picked, axis=1)
        x, y, z = (asked[j : j + 1] for j in (1, 2, 3))
        ax = jnp.where((corner & 1) != 0, x, 1.0 - x)
        ay = jnp.where((corner & 2) != 0, y, 1.0 - y)
        az = jnp.where((corner & 4) != 0, z, 1.0 - z)
        values = jnp.exp(-2.0 * jnp.sum(ax * ay * az * chosen, axis=0, keepdims=True))
        for j in range(group):
            answer[first + j] = values[:, j * cap : (j + 1) * cap]
        for j in range(1, group):
            reply(j)
        pl.when(g > 0)(functools.partial(reply, 0))
        return carry

    lax.fori_loop(0, n // group, serve, 0)
    found[me] = answer[0]

    for copy in local[5:]:
        copy.wait()
    for copy in halo:
        copy.wait()
    fld[...] = jnp.zeros_like(fld)
    for c in range(3):
        for z in range(nz - 1):
            fld[c, z, 0 : ny - 1, :] = disp[c, z]
            fld[c, z, ny - 1 : ny, :] = hy[c, z : z + 1, :]
        fld[c, nz - 1, 0 : ny - 1, :] = hz[c]
        fld[c, nz - 1, ny - 1 : ny, :] = hc[c : c + 1, :]

    def derivatives(flat):
        along = dot(split(flat, 1), xt[...])
        result = []
        for c in range(3):
            rows = along[c * nz * ROW : (c + 1) * nz * ROW]
            dx = dot(vv[...], split(rows[:, qxp:], 0))
            dyz = dot(vdv[...], split(rows[:, :qxp], 0))
            result.append([dx, dyz[:qrp], dyz[qrp:]])
        return result

    jac = derivatives(fld[...].reshape(3 * nz * ROW, -1))
    for c in range(3):
        jac[c][c] = jac[c][c] + 1.0

    wait_bytes(found.at[pl.ds(0, n - 1)], f_recv)
    scat[...] = jnp.zeros_like(scat)
    hi_rows = lax.broadcasted_iota(jnp.int32, (qrp, wide), 0)

    def place(g, carry):
        first = g * group
        p = jnp.concatenate([point[pl.ds(first + j, 1), :] for j in range(group)], axis=1)
        level = jnp.floor((p.astype(jnp.float32) + 0.5) * (1.0 / qx)).astype(jnp.int32)
        mine = hi_rows == level
        value = jnp.concatenate([found[first + j] for j in range(group)], axis=1)
        pieces = []
        for _ in range(3):
            piece = value.astype(jnp.bfloat16).astype(jnp.float32)
            value = value - piece
            pieces.append(jnp.where(mine, piece, 0.0))
        left = jnp.concatenate(pieces, axis=0).astype(jnp.bfloat16)
        scat[...] += dot(left, spots[g])
        return carry

    lax.fori_loop(0, n // group, place, 0)
    scale = scat[:qrp] + scat[qrp : 2 * qrp] + scat[2 * qrp :]
    weights = wts[...]
    scale = jnp.where(weights > 0.0, scale, 0.0)

    pairs = [(k, l) for k in range(3) for l in range(k, 3)]

    def gram(a, b):
        return {
            (k, l): a[0][k] * b[0][l] + a[1][k] * b[1][l] + a[2][k] * b[2][l]
            for k, l in (pairs if a is b else [(k, l) for k in range(3) for l in range(3)])
        }

    def inner(a, b):
        diag = sum(a[k, k] * b[k, k] for k in range(3))
        off = a[0, 1] * b[0, 1] + a[0, 2] * b[0, 2] + a[1, 2] * b[1, 2]
        return jnp.sum(weights * (diag + 2.0 * off), axis=0, keepdims=True)

    for turn in range(PASSES):
        gr = gram(jac, jac)
        r0 = {kl: gr[kl] * scale - (1.0 if kl[0] == kl[1] else 0.0) for kl in pairs}
        factor = (4.0 * weights) * scale
        across = []
        for c in range(3):
            pulled = []
            for k in range(3):
                total = sum(r0[min(k, l), max(k, l)] * jac[c][l] for l in range(3))
                pulled.append(total * factor)
            by_value = dot(vdvt[...], split(jnp.concatenate([pulled[1], pulled[2]], axis=0), 0))
            by_slope = dot(vvt[...], split(pulled[0], 0))
            across.append(jnp.concatenate([by_value, by_slope], axis=1))
        node = dot(split(jnp.concatenate(across, axis=0), 1), xtt[...])
        grad[turn] = node.reshape(3, nz, ROW, -1)

        for c in range(3):
            for side, y in enumerate((0, ny - 1)):
                for z in range(nz):
                    ysend[turn, side, c, z : z + 1, :] = grad[turn, c, z, y : y + 1, :]
                for zside, z in enumerate((0, nz - 1)):
                    csend[turn, 2 * zside + side, c : c + 1, :] = grad[turn, c, z, y : y + 1, :]
        copies = []
        for side, step in enumerate((-1, 1)):
            plane = (0, nz - 1)[side]
            copies.append((grad.at[turn, :, plane], zrecv.at[turn, 1 - side], near(step, 0)))
            copies.append((ysend.at[turn, side], yrecv.at[turn, 1 - side], near(0, step)))
            for other, ystep in enumerate((-1, 1)):
                index = 2 * side + other
                copies.append((csend.at[turn, index], crecv.at[turn, 3 - index], near(step, ystep)))
        copies = [
            remote(src, dst, x_send.at[8 * turn + i], x_recv.at[8 * turn + i], target)
            for i, (src, dst, target) in enumerate(copies)
        ]
        for copy in copies:
            copy.start()
        for copy in copies:
            copy.wait()
        for c in range(3):
            for side, z in enumerate((0, nz - 1)):
                grad[turn, c, z] += zrecv[turn, side, c]
            for side, y in enumerate((0, ny - 1)):
                for z in range(nz):
                    grad[turn, c, z, y : y + 1, :] += yrecv[turn, side, c, z : z + 1, :]
                for zside, z in enumerate((0, nz - 1)):
                    grad[turn, c, z, y : y + 1, :] += crecv[turn, 2 * zside + side, c : c + 1, :]

        direction = -grad[turn]
        move = derivatives(direction.reshape(3 * nz * ROW, -1))
        mixed = gram(jac, move)
        r1 = {(k, l): (mixed[k, l] + mixed[l, k]) * scale for k, l in pairs}
        mm = gram(move, move)
        r2 = {kl: mm[kl] * scale for kl in pairs}
        terms = [
            inner(r0, r0), inner(r0, r1), inner(r0, r2),
            inner(r1, r2), inner(r2, r2), inner(r1, r1),
        ]
        terms = jnp.concatenate(terms + [jnp.zeros((2, qxp), jnp.float32)], axis=0)
        mine = terms[:, :128]
        for lane in range(128, qxp, 128):
            mine = mine + terms[:, lane : lane + 128]
        part[turn] = mine
        sums[turn, me] = mine

        def share(slot, index, target, turn=turn):
            remote(
                part.at[turn], sums.at[turn, me], a_send.at[turn], a_recv.at[turn], target
            ).start()

        each_partner(share)
        wait_bytes(sums.at[turn, pl.ds(0, n - 1)], a_recv.at[turn])
        totals = jnp.sum(jnp.sum(sums[turn], axis=0), axis=1, keepdims=True)
        d00, d01, d02, d12, d22, gn = (
            jnp.broadcast_to(totals[i : i + 1], (1, 128)) for i in range(6)
        )
        c0, c1, c2, c3, c4 = d00, 2.0 * d01, gn + 2.0 * d02, 2.0 * d12, d22
        t = jnp.zeros((1, 128), jnp.float32)
        for _ in range(LS_STEPS):
            slope = c1 + t * (2.0 * c2 + t * (3.0 * c3 + t * 4.0 * c4))
            curvature = 2.0 * c2 + t * (6.0 * c3 + t * 12.0 * c4)
            t = t - slope / jnp.maximum(curvature, gn + 1e-06)
        count = n * (qrp // 9) * (qx // 3)
        for i, value in enumerate((c0, c1, c2, c3, c4)):
            lc[turn : turn + 1, i : i + 1] = value[:, :1] / count
        fld[...] = fld[...] + t.reshape(1, 1, 1, 128) * direction
        if turn + 1 < PASSES:
            step = t[:, :1]
            jac = [[jac[c][k] + step * move[c][k] for k in range(3)] for c in range(3)]

    for c in range(3):
        for z in range(nz - 1):
            at = (c * (nz - 1) + z) * (ny - 1)
            out[at : at + ny - 1, :] = fld[c, z, 0 : ny - 1, :]

    wait_bytes(query.at[pl.ds(0, n - 1)], q_send)
    wait_bytes(answer.at[pl.ds(0, n - 1)], f_send)
    for turn in range(PASSES):
        wait_bytes(sums.at[turn, pl.ds(0, n - 1)], a_send.at[turn])


def shards(mesh_shape, displacement, bg_coef, query_elem, query_point, query_coord):
    n_mesh, n_bg = mesh_shape
    n = n_mesh * n_bg
    _, nz0, ny0, nx = displacement.shape
    ze, ye, xe = nz0 // 2, ny0 // 2, nx // 2
    nz, ny = nz0 + 1, ny0 + 1
    assert ny <= ROW and nx == 128
    cap = query_elem.shape[2]
    tables = make_tables(ze, ye, xe)
    qrp, qxp = tables[-1].shape
    his = bg_coef.shape[1] // LO
    f32 = jnp.float32
    dims = (n_mesh, n_bg, nz, ny, 3 * xe)
    vmem = pl.BlockSpec(memory_space=pltpu.VMEM)
    dma = pltpu.SemaphoreType.DMA
    operands = (
        displacement, bg_coef, query_elem[0], query_point[0],
        jnp.transpose(query_coord[0], (1, 0, 2)),
        *(jnp.asarray(t) for t in tables),
    )
    scratch = [
        *(pltpu.VMEM(x.shape, x.dtype) for x in operands),
        pltpu.VMEM((n, 4, cap), f32),
        pltpu.VMEM((n, 4, cap), f32),
        pltpu.VMEM((n, 1, cap), f32),
        pltpu.VMEM((n, 1, cap), f32),
        pltpu.VMEM((8 * his, 2 * LO), jnp.bfloat16),
        pltpu.VMEM((n_mesh, n_bg * cap, qxp), jnp.bfloat16),
        pltpu.VMEM((3 * qrp, qxp), f32),
        pltpu.VMEM((3, nz, ROW, nx), f32),
        pltpu.VMEM((PASSES, 3, nz, ROW, nx), f32),
        pltpu.VMEM((3, nz0, nx), f32),
        pltpu.VMEM((3, nx), f32),
        pltpu.VMEM((3, ny0, nx), f32),
        pltpu.VMEM((3, nz0, nx), f32),
        pltpu.VMEM((3, nx), f32),
        pltpu.VMEM((PASSES, 2, 3, nz, nx), f32),
        pltpu.VMEM((PASSES, 4, 3, nx), f32),
        pltpu.VMEM((PASSES, 2, 3, ROW, nx), f32),
        pltpu.VMEM((PASSES, 2, 3, nz, nx), f32),
        pltpu.VMEM((PASSES, 4, 3, nx), f32),
        pltpu.VMEM((PASSES, 8, 128), f32),
        pltpu.VMEM((PASSES, n, 8, 128), f32),
        dma((12,)), dma, dma((n,)), dma, dma, dma((3,)), dma((3,)),
        dma((8 * PASSES,)), dma((8 * PASSES,)), dma((PASSES,)), dma((PASSES,)),
    ]
    out, lc = pl.pallas_call(
        functools.partial(kernel, dims),
        out_shape=(
            jax.ShapeDtypeStruct((3 * nz0 * ny0, nx), f32),
            jax.ShapeDtypeStruct((PASSES, 5), f32),
        ),
        in_specs=[pl.BlockSpec(memory_space=pltpu.HBM)] * 12,
        out_specs=(vmem, vmem),
        scratch_shapes=scratch,
        compiler_params=pltpu.CompilerParams(
            collective_id=0, has_side_effects=True, vmem_limit_bytes=56 * 2**20
        ),
    )(*operands)
    return out.reshape(displacement.shape), lc


def solution(mesh):
    in_specs = (
        P(None, "mesh", "bg", None),
        P(None, ("mesh", "bg")),
        P(("mesh", "bg"), None, None),
        P(("mesh", "bg"), None, None),
        P(("mesh", "bg"), None, None, None),
    )
    out_specs = (P(None, "mesh", "bg", None), P())
    body = functools.partial(shards, (mesh.shape["mesh"], mesh.shape["bg"]))
    return jax.shard_map(body, mesh=mesh, in_specs=in_specs, out_specs=out_specs, check_vma=False)
```

```python
import functools

import jax
import jax.numpy as jnp
import ml_dtypes
import numpy as np
from jax import lax
from jax.experimental import pallas as pl
from jax.experimental.pallas import tpu as pltpu
from jax.sharding import PartitionSpec as P

PASSES = 2
LS_STEPS = 4
ROW = 8
LO = 256
CHUNK = 768

GAUSS_POINTS = np.array([0.5 - 0.5 * np.sqrt(0.6), 0.5, 0.5 + 0.5 * np.sqrt(0.6)])
GAUSS_WEIGHTS = np.array([5.0 / 18.0, 8.0 / 18.0, 5.0 / 18.0])
MESH = pl.DeviceIdType.MESH


def basis_tables(elements, periodic):
    node_count = 2 * elements if periodic else 2 * elements + 1
    values = np.zeros((node_count, 3 * elements))
    slopes = np.zeros((node_count, 3 * elements))
    points = GAUSS_POINTS
    shape_values = [
        2.0 * (points - 0.5) * (points - 1.0),
        -4.0 * points * (points - 1.0),
        2.0 * points * (points - 0.5),
    ]
    shape_slopes = [4.0 * points - 3.0, 4.0 - 8.0 * points, 4.0 * points - 1.0]
    for offset in range(3):
        node_rows = (2 * np.arange(elements) + offset) % node_count
        for gauss_index in range(3):
            columns = 3 * np.arange(elements) + gauss_index
            values[node_rows, columns] += shape_values[offset][gauss_index]
            slopes[node_rows, columns] += shape_slopes[offset][gauss_index]
    return values, slopes


def round_up(value, unit):
    return -(-value // unit) * unit


def make_tables(ze, ye, xe):
    zv, zs = basis_tables(ze, False)
    yv, ys = basis_tables(ye, False)
    xv, xs = basis_tables(xe, True)
    nz, ny = zv.shape[0], yv.shape[0]
    qr, qx = 9 * ze * ye, 3 * xe
    qrp, qxp = round_up(qr, 8), round_up(qx, 128)

    def rows(tz, ty):
        out = np.zeros((qrp, nz, ROW))
        out[:qr, :, :ny] = np.einsum("zk,yl->klzy", tz, ty).reshape(qr, nz, ny)
        return out.reshape(qrp, nz * ROW)

    vv, vd, dv = rows(zv, yv), rows(zv, ys), rows(zs, yv)
    along_x = np.zeros((2 * xe, 2 * qxp))
    along_x[:, :qx] = xv
    along_x[:, qxp : qxp + qx] = xs
    weights = np.zeros((qrp, qxp))
    weights[:qr, :qx] = np.einsum(
        "z,y,x->zyx",
        np.tile(GAUSS_WEIGHTS, ze),
        np.tile(GAUSS_WEIGHTS, ye),
        np.tile(GAUSS_WEIGHTS, xe),
    ).reshape(qr, qx)
    return (
        thirds(along_x, 0),
        thirds(along_x.T, 0),
        thirds(vv, 1),
        thirds(np.concatenate([vd, dv], axis=0), 1),
        thirds(vv.T, 1),
        thirds(np.concatenate([vd.T, dv.T], axis=1), 1),
        weights.astype(np.float32),
    )


def thirds(table, axis):
    head = table.astype(ml_dtypes.bfloat16)
    tail = (table - head.astype(np.float64)).astype(ml_dtypes.bfloat16)
    return np.concatenate([head, head, tail], axis=axis)


def split(value, axis):
    head = value.astype(jnp.bfloat16).astype(jnp.float32)
    return jnp.concatenate([head, value - head, head], axis=axis).astype(jnp.bfloat16)


def dot(a, b):
    return lax.dot_general(
        a, b, (((1,), (0,)), ((), ())), preferred_element_type=jnp.float32
    )


def kernel(
    dims,
    disp_in, coef_in, elem_in, point_in, coord_in,
    xt_in, xtt_in, vv_in, vdv_in, vvt_in, vdvt_in, wts_in,
    out, lc,
    disp, coef, elem, point, coord, xt, xtt, vv, vdv, vvt, vdvt, wts,
    query, arrived, answer, found, tab, spots, scat, fld, grad,
    hy_send, hc_send, hz, hy, hc,
    ysend, csend, zrecv, yrecv, crecv, part, sums,
    l_sem, q_send, q_recv, f_send, f_recv, h_send, h_recv, x_send, x_recv, a_send, a_recv,
):
    n_mesh, n_bg, nz, ny, qx = dims
    n = n_mesh * n_bg
    cap = elem.shape[1]
    his = coef.shape[1] // LO
    qrp, qxp = wts.shape
    zi, yi = lax.axis_index("mesh"), lax.axis_index("bg")
    me = zi * n_bg + yi

    group = n_bg
    ahead = [lax.rem(yi + dy, n_bg) for dy in range(n_bg)]
    behind = [lax.rem(yi + (n_bg - dy), n_bg) for dy in range(n_bg)]

    def each_partner(act):
        for dy in range(1, n_bg):
            act(dy, zi * n_bg + ahead[dy], (zi, ahead[dy]))

        def row(dz, carry):
            z = lax.rem(zi + dz, n_mesh)
            for dy in range(n_bg):
                act(dz * n_bg + dy, z * n_bg + ahead[dy], (z, ahead[dy]))
            return carry

        lax.fori_loop(1, n_mesh, row, 0)

    def near(dz, dy):
        return (lax.rem(zi + n_mesh + dz, n_mesh), lax.rem(yi + n_bg + dy, n_bg))

    def remote(src, dst, ssem, rsem, target):
        return pltpu.make_async_remote_copy(
            src_ref=src, dst_ref=dst, send_sem=ssem, recv_sem=rsem,
            device_id=target, device_id_type=MESH,
        )

    def wait_bytes(ref, sem):
        pltpu.make_async_copy(ref, ref, sem).wait()

    local = [
        pltpu.make_async_copy(src, dst, l_sem.at[i])
        for i, (src, dst) in enumerate(
            (
                (elem_in, elem), (coord_in, coord), (disp_in, disp), (point_in, point),
                (coef_in, coef), (xt_in, xt), (xtt_in, xtt), (vv_in, vv), (vdv_in, vdv),
                (vvt_in, vvt), (vdvt_in, vdvt), (wts_in, wts),
            )
        )
    ]
    for copy in local:
        copy.start()
    barrier = pltpu.get_barrier_semaphore()

    def greet(slot, index, target):
        pl.semaphore_signal(barrier, inc=1, device_id=target, device_id_type=MESH)

    each_partner(greet)
    for copy in local[:3]:
        copy.wait()

    def pack(o, carry):
        query[o, 0:1, :] = elem[pl.ds(o, 1), :].astype(jnp.float32)
        for j in range(3):
            query[o, 1 + j : 2 + j, :] = coord[j, pl.ds(o, 1), :]
        return carry

    lax.fori_loop(0, n, pack, 0)
    for c in range(3):
        for z in range(nz - 1):
            hy_send[c, z : z + 1, :] = disp[c, z, 0:1, :]
        hc_send[c : c + 1, :] = disp[c, 0, 0:1, :]
    pl.semaphore_wait(barrier, n - 1)

    def send_query(slot, index, target):
        remote(query.at[index], arrived.at[slot], q_send, q_recv.at[slot], target).start()

    each_partner(send_query)
    halo = [
        remote(disp.at[:, 0], hz, h_send.at[0], h_recv.at[0], near(-1, 0)),
        remote(hy_send, hy, h_send.at[1], h_recv.at[1], near(0, -1)),
        remote(hc_send, hc, h_send.at[2], h_recv.at[2], near(-1, -1)),
    ]
    for copy in halo:
        copy.start()

    local[3].wait()
    one, zero = jnp.bfloat16(1.0), jnp.bfloat16(0.0)
    qx_lanes = lax.broadcasted_iota(jnp.int32, (group * cap, qxp), 1).astype(jnp.bfloat16)
    places = point[...].astype(jnp.float32)
    levels = jnp.floor((places + 0.5) * (1.0 / qx))
    offsets = jnp.transpose(places - levels * qx)
    for g in range(n // group):
        column = jnp.concatenate(
            [offsets[:, group * g + j : group * g + j + 1] for j in range(group)], axis=0
        ).astype(jnp.bfloat16)
        spots[g] = jnp.where(qx_lanes == column, one, zero)

    local[4].wait()
    for h in range(0, his, 2):
        pair = jnp.concatenate(
            [coef[:, LO * h : LO * (h + 1)], coef[:, LO * (h + 1) : LO * (h + 2)]], axis=0
        )
        top = pair.astype(jnp.bfloat16)
        tab[8 * h : 8 * h + 16, :LO] = top
        tab[8 * h : 8 * h + 16, LO:] = (pair - top.astype(jnp.float32)).astype(jnp.bfloat16)
    arrived[0] = query[me]

    wide = group * cap
    corner = lax.broadcasted_iota(jnp.int32, (8, wide), 0)
    lo_rows = lax.broadcasted_iota(jnp.int32, (LO, wide), 0).astype(jnp.bfloat16)

    def serve(g, carry):
        first = g * group
        back = lax.rem(zi + (n_mesh - g), n_mesh)

        def await_query(j):
            d = first + j
            remote(
                query.at[0], arrived.at[d], q_send, q_recv.at[d], (back, behind[j])
            ).wait_recv()

        def reply(j):
            remote(
                answer.at[first + j], found.at[me], f_send, f_recv, (back, behind[j])
            ).start()

        for j in range(1, group):
            await_query(j)
        pl.when(g > 0)(functools.partial(await_query, 0))

        asked = jnp.concatenate([arrived[first + j] for j in range(group)], axis=1)
        ids = asked[0:1].astype(jnp.int32)
        hi = lax.shift_right_logical(ids, LO.bit_length() - 1)
        lo = lax.bitwise_and(ids, LO - 1).astype(jnp.float32).astype(jnp.bfloat16)
        picked = []
        for at in range(0, wide, CHUNK):
            end = min(at + CHUNK, wide)
            one_hot = jnp.where(lo_rows[:, at:end] == lo[:, at:end], one, zero)
            rows = dot(tab[...], jnp.concatenate([one_hot, one_hot], axis=0))
            hi8 = jnp.broadcast_to(hi[:, at:end], (8, end - at))
            chosen = rows[0:8]
            for h in range(1, his):
                chosen = jnp.where(hi8 == h, rows[8 * h : 8 * h + 8], chosen)
            picked.append(chosen)
        chosen = jnp.concatenate(picked, axis=1)
        x, y, z = (asked[j : j + 1] for j in (1, 2, 3))
        ax = jnp.where((corner & 1) != 0, x, 1.0 - x)
        ay = jnp.where((corner & 2) != 0, y, 1.0 - y)
        az = jnp.where((corner & 4) != 0, z, 1.0 - z)
        values = jnp.exp(-2.0 * jnp.sum(ax * ay * az * chosen, axis=0, keepdims=True))
        for j in range(group):
            answer[first + j] = values[:, j * cap : (j + 1) * cap]
        for j in range(1, group):
            reply(j)
        pl.when(g > 0)(functools.partial(reply, 0))
        return carry

    lax.fori_loop(0, n // group, serve, 0)
    found[me] = answer[0]

    for copy in local[5:]:
        copy.wait()
    for copy in halo:
        copy.wait()
    fld[...] = jnp.zeros_like(fld)
    for c in range(3):
        for z in range(nz - 1):
            fld[c, z, 0 : ny - 1, :] = disp[c, z]
            fld[c, z, ny - 1 : ny, :] = hy[c, z : z + 1, :]
        fld[c, nz - 1, 0 : ny - 1, :] = hz[c]
        fld[c, nz - 1, ny - 1 : ny, :] = hc[c : c + 1, :]

    def derivatives(flat):
        along = dot(split(flat, 1), xt[...])
        result = []
        for c in range(3):
            rows = along[c * nz * ROW : (c + 1) * nz * ROW]
            dx = dot(vv[...], split(rows[:, qxp:], 0))
            dyz = dot(vdv[...], split(rows[:, :qxp], 0))
            result.append([dx, dyz[:qrp], dyz[qrp:]])
        return result

    jac = derivatives(fld[...].reshape(3 * nz * ROW, -1))
    for c in range(3):
        jac[c][c] = jac[c][c] + 1.0

    wait_bytes(found.at[pl.ds(0, n - 1)], f_recv)
    scat[...] = jnp.zeros_like(scat)
    hi_rows = lax.broadcasted_iota(jnp.int32, (qrp, wide), 0)

    def place(g, carry):
        first = g * group
        p = jnp.concatenate([point[pl.ds(first + j, 1), :] for j in range(group)], axis=1)
        level = jnp.floor((p.astype(jnp.float32) + 0.5) * (1.0 / qx)).astype(jnp.int32)
        mine = hi_rows == level
        value = jnp.concatenate([found[first + j] for j in range(group)], axis=1)
        pieces = []
        for _ in range(2):
            piece = value.astype(jnp.bfloat16).astype(jnp.float32)
            value = value - piece
            pieces.append(jnp.where(mine, piece, 0.0))
        left = jnp.concatenate(pieces, axis=0).astype(jnp.bfloat16)
        scat[...] += dot(left, spots[g])
        return carry

    lax.fori_loop(0, n // group, place, 0)
    scale = scat[:qrp] + scat[qrp:]
    weights = wts[...]
    scale = jnp.where(weights > 0.0, scale, 0.0)

    pairs = [(k, l) for k in range(3) for l in range(k, 3)]

    def gram(a, b):
        return {
            (k, l): a[0][k] * b[0][l] + a[1][k] * b[1][l] + a[2][k] * b[2][l]
            for k, l in (pairs if a is b else [(k, l) for k in range(3) for l in range(3)])
        }

    def inner(a, b):
        diag = sum(a[k, k] * b[k, k] for k in range(3))
        off = a[0, 1] * b[0, 1] + a[0, 2] * b[0, 2] + a[1, 2] * b[1, 2]
        return jnp.sum(weights * (diag + 2.0 * off), axis=0, keepdims=True)

    for turn in range(PASSES):
        gr = gram(jac, jac)
        r0 = {kl: gr[kl] * scale - (1.0 if kl[0] == kl[1] else 0.0) for kl in pairs}
        factor = (4.0 * weights) * scale
        across = []
        for c in range(3):
            pulled = []
            for k in range(3):
                total = sum(r0[min(k, l), max(k, l)] * jac[c][l] for l in range(3))
                pulled.append(total * factor)
            by_value = dot(vdvt[...], split(jnp.concatenate([pulled[1], pulled[2]], axis=0), 0))
            by_slope = dot(vvt[...], split(pulled[0], 0))
            across.append(jnp.concatenate([by_value, by_slope], axis=1))
        node = dot(split(jnp.concatenate(across, axis=0), 1), xtt[...])
        grad[turn] = node.reshape(3, nz, ROW, -1)

        for c in range(3):
            for side, y in enumerate((0, ny - 1)):
                for z in range(nz):
                    ysend[turn, side, c, z : z + 1, :] = grad[turn, c, z, y : y + 1, :]
                for zside, z in enumerate((0, nz - 1)):
                    csend[turn, 2 * zside + side, c : c + 1, :] = grad[turn, c, z, y : y + 1, :]
        copies = []
        for side, step in enumerate((-1, 1)):
            plane = (0, nz - 1)[side]
            copies.append((grad.at[turn, :, plane], zrecv.at[turn, 1 - side], near(step, 0)))
            copies.append((ysend.at[turn, side], yrecv.at[turn, 1 - side], near(0, step)))
            for other, ystep in enumerate((-1, 1)):
                index = 2 * side + other
                copies.append((csend.at[turn, index], crecv.at[turn, 3 - index], near(step, ystep)))
        copies = [
            remote(src, dst, x_send.at[8 * turn + i], x_recv.at[8 * turn + i], target)
            for i, (src, dst, target) in enumerate(copies)
        ]
        for copy in copies:
            copy.start()
        for copy in copies:
            copy.wait()
        for c in range(3):
            for side, z in enumerate((0, nz - 1)):
                grad[turn, c, z] += zrecv[turn, side, c]
            for side, y in enumerate((0, ny - 1)):
                for z in range(nz):
                    grad[turn, c, z, y : y + 1, :] += yrecv[turn, side, c, z : z + 1, :]
                for zside, z in enumerate((0, nz - 1)):
                    grad[turn, c, z, y : y + 1, :] += crecv[turn, 2 * zside + side, c : c + 1, :]

        direction = -grad[turn]
        move = derivatives(direction.reshape(3 * nz * ROW, -1))
        mixed = gram(jac, move)
        r1 = {(k, l): (mixed[k, l] + mixed[l, k]) * scale for k, l in pairs}
        mm = gram(move, move)
        r2 = {kl: mm[kl] * scale for kl in pairs}
        terms = [
            inner(r0, r0), inner(r0, r1), inner(r0, r2),
            inner(r1, r2), inner(r2, r2), inner(r1, r1),
        ]
        terms = jnp.concatenate(terms + [jnp.zeros((2, qxp), jnp.float32)], axis=0)
        mine = terms[:, :128]
        for lane in range(128, qxp, 128):
            mine = mine + terms[:, lane : lane + 128]
        part[turn] = mine
        sums[turn, me] = mine

        def share(slot, index, target, turn=turn):
            remote(
                part.at[turn], sums.at[turn, me], a_send.at[turn], a_recv.at[turn], target
            ).start()

        each_partner(share)
        wait_bytes(sums.at[turn, pl.ds(0, n - 1)], a_recv.at[turn])
        totals = jnp.sum(jnp.sum(sums[turn], axis=0), axis=1, keepdims=True)
        d00, d01, d02, d12, d22, gn = (
            jnp.broadcast_to(totals[i : i + 1], (1, 128)) for i in range(6)
        )
        c0, c1, c2, c3, c4 = d00, 2.0 * d01, gn + 2.0 * d02, 2.0 * d12, d22
        t = jnp.zeros((1, 128), jnp.float32)
        for _ in range(LS_STEPS):
            slope = c1 + t * (2.0 * c2 + t * (3.0 * c3 + t * 4.0 * c4))
            curvature = 2.0 * c2 + t * (6.0 * c3 + t * 12.0 * c4)
            t = t - slope / jnp.maximum(curvature, gn + 1e-06)
        count = n * (qrp // 9) * (qx // 3)
        for i, value in enumerate((c0, c1, c2, c3, c4)):
            lc[turn : turn + 1, i : i + 1] = value[:, :1] / count
        fld[...] = fld[...] + t.reshape(1, 1, 1, 128) * direction
        if turn + 1 < PASSES:
            step = t[:, :1]
            jac = [[jac[c][k] + step * move[c][k] for k in range(3)] for c in range(3)]

    for c in range(3):
        for z in range(nz - 1):
            at = (c * (nz - 1) + z) * (ny - 1)
            out[at : at + ny - 1, :] = fld[c, z, 0 : ny - 1, :]

    wait_bytes(query.at[pl.ds(0, n - 1)], q_send)
    wait_bytes(answer.at[pl.ds(0, n - 1)], f_send)
    for turn in range(PASSES):
        wait_bytes(sums.at[turn, pl.ds(0, n - 1)], a_send.at[turn])


def shards(mesh_shape, displacement, bg_coef, query_elem, query_point, query_coord):
    n_mesh, n_bg = mesh_shape
    n = n_mesh * n_bg
    _, nz0, ny0, nx = displacement.shape
    ze, ye, xe = nz0 // 2, ny0 // 2, nx // 2
    nz, ny = nz0 + 1, ny0 + 1
    assert ny <= ROW and nx == 128
    cap = query_elem.shape[2]
    tables = make_tables(ze, ye, xe)
    qrp, qxp = tables[-1].shape
    his = bg_coef.shape[1] // LO
    f32 = jnp.float32
    dims = (n_mesh, n_bg, nz, ny, 3 * xe)
    vmem = pl.BlockSpec(memory_space=pltpu.VMEM)
    dma = pltpu.SemaphoreType.DMA
    operands = (
        displacement, bg_coef, query_elem[0], query_point[0],
        jnp.transpose(query_coord[0], (1, 0, 2)),
        *(jnp.asarray(t) for t in tables),
    )
    scratch = [
        *(pltpu.VMEM(x.shape, x.dtype) for x in operands),
        pltpu.VMEM((n, 4, cap), f32),
        pltpu.VMEM((n, 4, cap), f32),
        pltpu.VMEM((n, 1, cap), f32),
        pltpu.VMEM((n, 1, cap), f32),
        pltpu.VMEM((8 * his, 2 * LO), jnp.bfloat16),
        pltpu.VMEM((n_mesh, n_bg * cap, qxp), jnp.bfloat16),
        pltpu.VMEM((2 * qrp, qxp), f32),
        pltpu.VMEM((3, nz, ROW, nx), f32),
        pltpu.VMEM((PASSES, 3, nz, ROW, nx), f32),
        pltpu.VMEM((3, nz0, nx), f32),
        pltpu.VMEM((3, nx), f32),
        pltpu.VMEM((3, ny0, nx), f32),
        pltpu.VMEM((3, nz0, nx), f32),
        pltpu.VMEM((3, nx), f32),
        pltpu.VMEM((PASSES, 2, 3, nz, nx), f32),
        pltpu.VMEM((PASSES, 4, 3, nx), f32),
        pltpu.VMEM((PASSES, 2, 3, ROW, nx), f32),
        pltpu.VMEM((PASSES, 2, 3, nz, nx), f32),
        pltpu.VMEM((PASSES, 4, 3, nx), f32),
        pltpu.VMEM((PASSES, 8, 128), f32),
        pltpu.VMEM((PASSES, n, 8, 128), f32),
        dma((12,)), dma, dma((n,)), dma, dma, dma((3,)), dma((3,)),
        dma((8 * PASSES,)), dma((8 * PASSES,)), dma((PASSES,)), dma((PASSES,)),
    ]
    out, lc = pl.pallas_call(
        functools.partial(kernel, dims),
        out_shape=(
            jax.ShapeDtypeStruct((3 * nz0 * ny0, nx), f32),
            jax.ShapeDtypeStruct((PASSES, 5), f32),
        ),
        in_specs=[pl.BlockSpec(memory_space=pltpu.HBM)] * 12,
        out_specs=(vmem, vmem),
        scratch_shapes=scratch,
        compiler_params=pltpu.CompilerParams(
            collective_id=0, has_side_effects=True, vmem_limit_bytes=56 * 2**20
        ),
    )(*operands)
    return out.reshape(displacement.shape), lc


def solution(mesh):
    in_specs = (
        P(None, "mesh", "bg", None),
        P(None, ("mesh", "bg")),
        P(("mesh", "bg"), None, None),
        P(("mesh", "bg"), None, None),
        P(("mesh", "bg"), None, None, None),
    )
    out_specs = (P(None, "mesh", "bg", None), P())
    body = functools.partial(shards, (mesh.shape["mesh"], mesh.shape["bg"]))
    return jax.shard_map(body, mesh=mesh, in_specs=in_specs, out_specs=out_specs, check_vma=False)
```
